256 devices in a mesh: sky: 32 (over y, x, core), gz: 8 (over z).
Axes of the slice: x: 4, y: 4, z: 8, core: 2. Of those that a mesh axis runs over, the one named last changes fastest.
Arguments:
- delta_flux: float32 [32, 8, 32, 128], P('sky', 'gz'), may hold values from -6 to 6
- noise_var: float32 [32, 8, 32, 128], P('sky', 'gz'), may hold values from 0.5 to 2
- pixel_pos: float32 [32, 8, 3, 32, 128], P('sky', 'gz'), may hold values from 0 to 64, as said below
- pixel_count: int32 [32, 8, 32], P('sky', 'gz'), may hold values from 1 to 128, as said below
- pair_list: int32 [32, 8, 3, 128], P('sky', 'gz'), may hold values from 0 to 31, as said below
Outputs:
- wiener_field: float32 [32, 8, 32, 128], P('sky', 'gz')
- residual: float32 [32, 8, 32, 128], P('sky', 'gz')
The draws below stay inside these ranges and needn't reach their ends.
Inputs may be any that keep to these rules, and one draw needn't show every extreme that they name: pair_list[t, g, 0, k] is a neighbour code 3 (a + 1) + (b + 1) for a sky offset a and a redshift offset b in -1..1, or 9 for an empty slot; rows 1 and 2 are block numbers below 32. On every tile the filled slots come first, sorted by code; their number differs from tile to tile and one tile fills all 128 slots. `pixel_count`: every tile and segment has a block with all 128 pixels live. `pixel_pos`: component 0 of tile t lies in [2 t, 2 t + 2], component 1 in [0, 2], component 2 of segment g in [4 g, 4 g + 4].
All inputs are finite; a program needn't handle non-finite values.
Results may differ from the reference program's by a relative error of at most 0.00075.
Values sent between devices are 32-bit elements; how exact they have to be, the bound alone decides.
A program may use at most 128 MiB of HBM per device.

```python
import math
import jax
import jax.numpy as jnp
from jax import lax

BLK = 128
NB = 32
ITERS = 3
PAIRS = 128
N_SKY = 32
N_GZ = 8


def draw_pair_list(key, part):
    key = jax.random.fold_in(key, 11)
    keys = jax.random.split(key, 6)
    quarter = PAIRS // 4
    remain = PAIRS - quarter
    first_r = jax.random.randint(keys[0], (N_SKY, N_GZ), 0, remain + 1)
    second_r = jax.random.randint(keys[1], (N_SKY, N_GZ), 0, remain + 1)
    filled = quarter + first_r * second_r // max(remain, 1)
    fullest = jax.random.randint(keys[2], (), 0, N_SKY * N_GZ)
    tile_ids = jnp.arange(N_SKY * N_GZ, dtype=jnp.int32).reshape(N_SKY, N_GZ)
    filled = jnp.where(tile_ids == fullest, PAIRS, filled)
    nbr_code = jax.random.randint(keys[3], (N_SKY, N_GZ, PAIRS), 0, 9)
    source = jax.random.randint(keys[4], (N_SKY, N_GZ, PAIRS), 0, NB)
    target = jax.random.randint(keys[5], (N_SKY, N_GZ, PAIRS), 0, NB)
    slots = jnp.arange(PAIRS, dtype=jnp.int32)
    keyed = jnp.where(slots[None, None, :] < filled[..., None], nbr_code, 9)
    order = jnp.argsort(keyed * PAIRS + slots[None, None, :], axis=-1)
    keyed = jnp.take_along_axis(keyed, order, axis=-1)
    source = jnp.take_along_axis(source, order, axis=-1)
    target = jnp.take_along_axis(target, order, axis=-1)
    return jnp.stack([keyed, source, target], axis=2).astype(jnp.int32)


def draw_pixel_count(key, part):
    key = jax.random.fold_in(key, 12)
    keys = jax.random.split(key, 2)
    counts = jax.random.randint(keys[0], (N_SKY, N_GZ, NB), 1, BLK + 1)
    fullest = jax.random.randint(keys[1], (N_SKY, N_GZ), 0, NB)
    blocks = jnp.arange(NB, dtype=jnp.int32)
    counts = jnp.where(blocks[None, None, :] == fullest[..., None], BLK, counts)
    return counts.astype(jnp.int32)


def draw_pixel_pos(key, part):
    key = jax.random.fold_in(key, 13)
    keys = jax.random.split(key, 3)
    skewers = BLK // 8
    off_x = jax.random.uniform(keys[0], (N_SKY, N_GZ, NB, skewers), jnp.float32, 0.0, 2.0)
    off_y = jax.random.uniform(keys[1], (N_SKY, N_GZ, NB, skewers), jnp.float32, 0.0, 2.0)
    jitter = jax.random.uniform(keys[2], (N_SKY, N_GZ, NB, BLK), jnp.float32, 0.0, 0.5)
    tile = jnp.arange(N_SKY, dtype=jnp.float32).reshape(N_SKY, 1, 1, 1)
    segment = jnp.arange(N_GZ, dtype=jnp.float32).reshape(1, N_GZ, 1, 1)
    coord_x = 2.0 * tile + jnp.repeat(off_x, 8, axis=-1)
    coord_y = jnp.repeat(off_y, 8, axis=-1)
    along = (jnp.arange(BLK, dtype=jnp.int32) % 8).astype(jnp.float32).reshape(1, 1, 1, BLK) * 0.5
    coord_z = 4.0 * segment + along + jitter
    return jnp.stack([coord_x, coord_y, coord_z], axis=2).astype(jnp.float32)


def block_scale(own_key, dims, cuts, low, top_value):
    level = 1.0
    for axis_at, parts in cuts:
        draws = jax.random.uniform(jax.random.fold_in(jax.random.fold_in(own_key, 6), axis_at), (parts,), jnp.float32, low / len(cuts), top_value / len(cuts))
        level = level * jnp.repeat(jnp.exp(draws), dims[axis_at] // parts).reshape((-1,) + (1,) * (len(dims) - 1 - axis_at))
    return level


def bell_draw(stream_key, shape, width, bound, cuts=(), kind=jnp.bfloat16):
    entries = jax.random.normal(stream_key, shape, jnp.float32) * width
    if len(cuts) > 0:
        entries = block_scale(stream_key, shape, cuts, -0.22, 0.18) * entries
    return jnp.clip(entries, min=-bound, max=bound).astype(kind)


def setup_inputs(seed: int = 0) -> dict:
    splits = jax.random.split(jax.random.key(seed), 6)
    return {
        "delta_flux": bell_draw(splits[0], (N_SKY, N_GZ, NB, BLK), 1.0, 6.0, ((0, 32), (1, 8)), jnp.float32),
        "noise_var": jnp.clip(jnp.exp(math.log(2.0) - 1.3862944 * jax.random.uniform(splits[1], (N_SKY, N_GZ, NB, BLK), jnp.float32) ** block_scale(splits[1], (N_SKY, N_GZ, NB, BLK), ((0, 32), (1, 8)), -0.2, 0.2)), 0.5, 2.0),
        "pixel_pos": draw_pixel_pos(jax.random.fold_in(splits[5], 71), 0),
        "pixel_count": draw_pixel_count(jax.random.fold_in(splits[5], 71), 0),
        "pair_list": draw_pair_list(jax.random.fold_in(splits[5], 71), 0),
    }


signal_amp = 0.25
spread_inv = 0.5


def kernel_tiles(left_pos, right_pos):
    diff_x = left_pos[:, 0, :, None] - right_pos[:, 0, None, :]
    diff_y = left_pos[:, 1, :, None] - right_pos[:, 1, None, :]
    diff_z = left_pos[:, 2, :, None] - right_pos[:, 2, None, :]
    squared = diff_x * diff_x + diff_y * diff_y + diff_z * diff_z
    return signal_amp * jnp.exp(-spread_inv * squared)


def apply_tiles(tiles, vectors):
    return jnp.einsum("gab,gb->ga", tiles, vectors, precision=lax.Precision.HIGHEST)


def apply_trans(tiles, vectors):
    return jnp.einsum("gab,ga->gb", tiles, vectors, precision=lax.Precision.HIGHEST)


def signal_apply(vector, pos_blocks, pair_list):
    n_tiles = N_SKY * N_GZ
    self_part = lax.map(
        lambda pieces: apply_tiles(kernel_tiles(pieces[0], pieces[0]), pieces[1]),
        (pos_blocks.reshape(n_tiles, NB, 3, BLK), vector.reshape(n_tiles, NB, BLK)),
    ).reshape(vector.shape)
    padded_vec = jnp.pad(vector, ((1, 1), (1, 1), (0, 0), (0, 0)))
    padded_pos = jnp.pad(pos_blocks, ((1, 1), (1, 1), (0, 0), (0, 0), (0, 0)))

    def visit(totals, device):
        tile_s = device // N_GZ
        tile_g = device % N_GZ
        entry = pair_list[tile_s, tile_g]
        nbr_code = entry[0]
        source = entry[1]
        target = entry[2]
        weight = (nbr_code < 9).astype(jnp.float32)[:, None]
        clipped = jnp.minimum(nbr_code, 8)
        row_s = tile_s + clipped // 3
        row_g = tile_g + clipped % 3
        far_pos = padded_pos[row_s, row_g, source]
        far_vec = padded_vec[row_s, row_g, source]
        near_pos = padded_pos[tile_s + 1, tile_g + 1, target]
        near_vec = padded_vec[tile_s + 1, tile_g + 1, target]
        cross_tile = kernel_tiles(near_pos, far_pos)
        to_target = weight * (apply_tiles(cross_tile, far_vec) + apply_tiles(kernel_tiles(near_pos, near_pos), near_vec))
        to_source = weight * (apply_trans(cross_tile, near_vec) + apply_tiles(kernel_tiles(far_pos, far_pos), far_vec))
        totals = totals.at[tile_s + 1, tile_g + 1, target].add(to_target)
        totals = totals.at[row_s, row_g, source].add(to_source)
        return totals, None

    totals = lax.scan(visit, jnp.zeros(padded_vec.shape, jnp.float32), jnp.arange(n_tiles, dtype=jnp.int32))[0]
    return self_part + totals[1:-1, 1:-1]


def reference(delta_flux, noise_var, pixel_pos, pixel_count, pair_list):
    pos_blocks = jnp.transpose(pixel_pos, (0, 1, 3, 2, 4))
    live_mask = (jnp.arange(BLK, dtype=jnp.int32)[None, None, None, :] < pixel_count[..., None]).astype(jnp.float32)
    precond = 1.0 / (noise_var + signal_amp)

    def operate(vector):
        return live_mask * signal_apply(vector, pos_blocks, pair_list) + noise_var * vector

    right_side = live_mask * delta_flux
    wiener_field = jnp.zeros_like(right_side)
    residual = right_side
    precond_res = precond * residual
    direction = precond_res
    rz_now = jnp.sum(residual * precond_res)
    for iteration in range(ITERS):
        image = operate(direction)
        step_len = rz_now / jnp.sum(direction * image)
        wiener_field = wiener_field + step_len * direction
        residual = residual - step_len * image
        precond_res = precond * residual
        rz_next = jnp.sum(residual * precond_res)
        direction = precond_res + (rz_next / rz_now) * direction
        rz_now = rz_next
    return wiener_field, residual
```

```python
import functools
import jax
import jax.numpy as jnp
from jax import lax
from jax.experimental import pallas as pl
from jax.experimental.pallas import tpu as pltpu
from jax.sharding import PartitionSpec as P

ITERS = 3
BLOCKS = 32
WIDTH = 128
CODES = 9
OWN = 4
SUB = 8
INNER = 8

signal_amp = 0.25
bf16 = jnp.bfloat16
f32 = jnp.float32


def mm(left, right):
    return lax.dot_general(left, right, (((1,), (0,)), ((), ())), preferred_element_type=f32)


def mm_trans(left, right):
    return lax.dot_general(left, right, (((1,), (1,)), ((), ())), preferred_element_type=f32)


def split_two(values):
    high = values.astype(bf16)
    return high, (values - high.astype(f32)).astype(bf16)


def split_three(values):
    high = values.astype(bf16).astype(f32)
    rest = values - high
    mid = rest.astype(bf16).astype(f32)
    return high, mid, rest - mid


def body(
    slots,
    delta_ref, noise_ref, pos_ref, count_ref, pair_ref, spair_ref,
    field_ref, resid_ref,
    near_ref, cov_ref, msg_ref, first_ref, halo1_ref, halo2_ref, owed_ref, got_ref,
    gain_ref, pay_ref, self_ref, basis_ref, image_ref, onto_ref, from_ref,
    sum_ref, red1_ref, red2_ref, red3_ref,
    first_send, first_recv, halo_send, halo_recv, owed_send, owed_recv,
    red1_send, red1_recv, red2_send, red2_recv, red3_send, red3_recv,
):
    n_sky = lax.axis_size("sky")
    n_gz = lax.axis_size("gz")
    n_outer = n_sky // INNER
    me_s = lax.axis_index("sky")
    me_g = lax.axis_index("gz")
    outer = me_s // INNER
    inner = me_s % INNER

    def tile_at(code):
        return (
            (me_s + code // 3 - 1 + n_sky) % n_sky,
            (me_g + code % 3 - 1 + n_gz) % n_gz,
        )

    def gz_at(step):
        return (me_s, (me_g + step) % n_gz)

    def inner_at(step):
        return (outer * INNER + (inner + step) % INNER, me_g)

    def outer_at(step):
        return ((outer + step) % n_outer * INNER + inner, me_g)

    sides = [code for code in range(CODES) if code != OWN]
    partners = [tile_at(code) for code in sides]
    partners += [gz_at(step) for step in range(1, n_gz)]
    partners += [inner_at(step) for step in range(1, INNER)]
    partners += [outer_at(step) for step in range(1, n_outer)]
    barrier = pltpu.get_barrier_semaphore()
    for partner in partners:
        pl.semaphore_signal(
            barrier, inc=1, device_id=partner, device_id_type=pl.DeviceIdType.MESH
        )

    def remote(source, target, send, recv, device):
        return pltpu.make_async_remote_copy(
            src_ref=source, dst_ref=target, send_sem=send, recv_sem=recv,
            device_id=device, device_id_type=pl.DeviceIdType.MESH,
        )

    eye_b = lax.broadcasted_iota(jnp.int32, (BLOCKS, BLOCKS), 0) == lax.broadcasted_iota(
        jnp.int32, (BLOCKS, BLOCKS), 1
    )
    count = jnp.sum(
        jnp.where(eye_b, count_ref[...].astype(f32), 0.0), axis=1, keepdims=True
    )
    lanes = lax.broadcasted_iota(jnp.int32, (BLOCKS, WIDTH), 1).astype(f32)
    live = (lanes < count).astype(f32)
    noise = noise_ref[...]
    precond = 1.0 / (noise + signal_amp)
    right_side = live * delta_ref[...]
    image_ref[0] = right_side
    basis_ref[0] = precond * right_side

    msg_ref[0 : 3 * BLOCKS] = pos_ref[...]
    msg_ref[3 * BLOCKS :] = basis_ref[0]
    pl.semaphore_wait(barrier, len(partners))
    first = [
        remote(msg_ref, first_ref.at[8 - c], first_send.at[c], first_recv.at[8 - c], tile_at(c))
        for c in sides
    ]
    for copy in first:
        copy.start()
    first_ref[OWN] = msg_ref[...]

    codes = pair_ref[0:1, :]
    near_row = (codes >= 3).astype(jnp.int32) + (codes >= 6).astype(jnp.int32)
    row_s = me_s + near_row - 1
    row_g = me_g + (codes - 3 * near_row) - 1
    filled = codes < CODES
    inside = filled & (row_s >= 0) & (row_s < n_sky) & (row_g >= 0) & (row_g < n_gz)
    flat = jnp.minimum(codes, CODES - 1) * BLOCKS + pair_ref[1:2, :]
    target = pair_ref[2:3, :]
    weight = jnp.where(inside, signal_amp, 0.0)
    rows_b = lax.broadcasted_iota(jnp.int32, (BLOCKS, slots), 0)
    hits = rows_b == target
    onto = jnp.where(hits, weight, 0.0)
    onto_ref[:, :slots] = onto.astype(bf16)
    onto_ref[:, slots:] = onto.astype(bf16)
    named = jnp.sum(
        jnp.where(hits & filled, signal_amp, 0.0), axis=1, keepdims=True
    )
    rows_f = lax.broadcasted_iota(jnp.int32, (CODES * BLOCKS, slots), 0)
    backs = jnp.where(rows_f == flat, weight, 0.0)
    from_ref[:, :slots] = backs.astype(bf16)
    from_ref[:, slots:] = backs.astype(bf16)
    sourced = jnp.broadcast_to(
        jnp.sum(backs, axis=1, keepdims=True), (CODES * BLOCKS, WIDTH)
    )
    for c in range(CODES):
        owed_ref[0, c, BLOCKS:] = sourced[c * BLOCKS : (c + 1) * BLOCKS]

    mid_x = (2 * me_s + 1).astype(f32)
    mid_z = (4 * me_g + 2).astype(f32)
    sub = lax.broadcasted_iota(jnp.int32, (SUB, WIDTH), 0)

    def features(code, block, swap):
        x = first_ref[code, pl.ds(block, 1), :] - mid_x
        y = first_ref[code, pl.ds(BLOCKS + block, 1), :] - 1.0
        z = first_ref[code, pl.ds(2 * BLOCKS + block, 1), :] - mid_z
        size = -0.5 * (x * x + y * y + z * z)
        tile = jnp.where(sub == 0, x, 0.0)
        tile = jnp.where(sub == 1, y, tile)
        tile = jnp.where(sub == 2, z, tile)
        tile = jnp.where(sub == (3 if swap else 4), size, tile)
        return jnp.where(sub == (4 if swap else 3), 1.0, tile)

    blank = jnp.zeros((WIDTH - 6 * SUB, WIDTH), f32)

    def near_step(block, _):
        h, m, l = split_three(features(OWN, block, True))
        stack = jnp.concatenate([h, h, m, m, h, l, blank], axis=0)
        near_ref[block] = jnp.transpose(stack).astype(bf16)
        return 0

    lax.fori_loop(0, BLOCKS, near_step, 0)

    def make_tile(slot, block, code, source):
        h, m, l = split_three(features(code, source, False))
        stack = jnp.concatenate([h, m, h, m, l, h, blank], axis=0).astype(bf16)
        values = jnp.exp(mm(near_ref[block], stack))
        high, low = split_two(values)
        cov_ref[slot, 0:WIDTH] = high
        cov_ref[slot, WIDTH:] = low

    def self_tile(step, _):
        for k in range(4):
            block = step * 4 + k
            make_tile(slots + block, block, OWN, block)
        return 0

    lax.fori_loop(0, BLOCKS // 4, self_tile, 0)
    for copy in first:
        copy.wait_recv()

    def pair_tile(step, _):
        for k in range(4):
            slot = step * 4 + k
            code = jnp.minimum(spair_ref[0, slot], CODES - 1)
            make_tile(slot, spair_ref[2, slot], code, spair_ref[1, slot])
        return 0

    lax.fori_loop(0, slots // 4, pair_tile, 0)

    def packed(rows):
        high, low = split_two(rows)
        return jnp.concatenate([high, low], axis=0)

    def doubled(values):
        high, low = split_two(values)
        return jnp.concatenate([high, low], axis=0)

    in_flight = []
    own_weight = None
    for it in range(ITERS):
        vector = basis_ref[it]
        if it == 0:
            arriving = []
            far_at = lambda code, block: first_ref[code, pl.ds(3 * BLOCKS + block, 1), :]
        else:
            halo_ref = (halo1_ref, halo2_ref)[it - 1]
            arriving = [
                remote(
                    basis_ref.at[it], halo_ref.at[8 - c],
                    halo_send.at[it - 1, c], halo_recv.at[it - 1, 8 - c], tile_at(c),
                )
                for c in sides
            ]
            for copy in arriving:
                copy.start()
            halo_ref[OWN] = vector
            far_at = functools.partial(
                lambda ref, code, block: ref[code, pl.ds(block, 1), :], halo_ref
            )

        def pay_step(step, _):
            rows = jnp.zeros((SUB, WIDTH), f32)
            for k in range(SUB):
                block = spair_ref[2, step * SUB + k]
                rows = jnp.where(sub == k, basis_ref[it, pl.ds(block, 1), :], rows)
            left = packed(rows)
            left = jnp.concatenate([left, left], axis=1)
            total = jnp.zeros((SUB, WIDTH), f32)
            for k in range(SUB):
                out = mm(left, cov_ref[step * SUB + k])
                total = jnp.where(sub == k, out[:SUB] + out[SUB:], total)
            pay_ref[pl.ds(step * SUB, SUB), :] = total
            return 0

        lax.fori_loop(0, slots // SUB, pay_step, 0)
        owed = mm(from_ref[...], doubled(pay_ref[...]))
        for c in range(CODES):
            owed_ref[it, c, 0:BLOCKS] = owed[c * BLOCKS : (c + 1) * BLOCKS]
        extent = 2 * BLOCKS if it == 0 else BLOCKS
        returns = [
            remote(
                owed_ref.at[it, c, pl.ds(0, extent)], got_ref.at[it, 8 - c, pl.ds(0, extent)],
                owed_send.at[it, c], owed_recv.at[it, 8 - c], tile_at(c),
            )
            for c in sides
        ]
        for copy in returns:
            copy.start()

        def self_step(step, _):
            left = packed(basis_ref[it, pl.ds(step * SUB, SUB), :])
            left = jnp.concatenate([left, left], axis=1)
            total = jnp.zeros((SUB, WIDTH), f32)
            for k in range(SUB):
                out = mm(left, cov_ref[slots + step * SUB + k])
                total = jnp.where(sub == k, out[:SUB] + out[SUB:], total)
            self_ref[pl.ds(step * SUB, SUB), :] = total
            return 0

        lax.fori_loop(0, BLOCKS // SUB, self_step, 0)
        for copy in arriving:
            copy.wait_recv()

        def gain_step(step, _):
            rows = jnp.zeros((SUB, WIDTH), f32)
            for k in range(SUB):
                slot = step * SUB + k
                code = jnp.minimum(spair_ref[0, slot], CODES - 1)
                rows = jnp.where(sub == k, far_at(code, spair_ref[1, slot]), rows)
            left = packed(rows)
            total = jnp.zeros((SUB, WIDTH), f32)
            for k in range(SUB):
                out = mm_trans(left, cov_ref[step * SUB + k])
                out = out[:SUB] + out[SUB:]
                total = jnp.where(sub == k, out[:, :WIDTH] + out[:, WIDTH:], total)
            gain_ref[pl.ds(step * SUB, SUB), :] = total
            return 0

        lax.fori_loop(0, slots // SUB, gain_step, 0)
        totals = mm(onto_ref[...], doubled(gain_ref[...])) + owed_ref[it, OWN, 0:BLOCKS]
        for copy in returns:
            copy.wait_recv()
        for c in sides:
            totals = totals + got_ref[it, c, 0:BLOCKS]
        if it == 0:
            own_weight = owed_ref[0, OWN, BLOCKS:] + (signal_amp + named)
            for c in sides:
                own_weight = own_weight + got_ref[0, c, BLOCKS:]
        totals = totals + own_weight * self_ref[...]
        image = live * totals + noise * vector
        image_ref[it + 1] = image
        basis_ref[it + 1] = precond * image
        in_flight += arriving + returns

    moments = jnp.zeros((SUB, WIDTH), f32)
    for m in range(2 * ITERS + 1):
        product = basis_ref[m // 2] * image_ref[m - m // 2]
        moments = jnp.where(sub == m, jnp.sum(product, axis=0, keepdims=True), moments)
    stages = (
        (gz_at, n_gz, red1_ref, red1_send, red1_recv),
        (inner_at, INNER, red2_ref, red2_send, red2_recv),
        (outer_at, n_outer, red3_ref, red3_send, red3_recv),
    )
    for stage, (device_at, members, into, send, recv) in enumerate(stages):
        sum_ref[stage] = moments
        copies = [
            remote(
                sum_ref.at[stage], into.at[step - 1], send.at[step - 1], recv.at[step - 1],
                device_at(step),
            )
            for step in range(1, members)
        ]
        for copy in copies:
            copy.start()
        for step, copy in enumerate(copies):
            copy.wait_recv()
            moments = moments + into[step]
        in_flight += copies
    total = jnp.sum(moments, axis=1, keepdims=True)
    mu = [total[m : m + 1] for m in range(2 * ITERS + 1)]

    def inner_product(left, right):
        value = None
        for i, a in enumerate(left):
            for j, b in enumerate(right):
                if a is not None and b is not None:
                    term = a * b * mu[i + j]
                    value = term if value is None else value + term
        return value

    def plus(left, scale, right):
        if right is None:
            return left
        return scale * right if left is None else left + scale * right

    one = jnp.ones((1, 1), f32)
    resid = [one, None, None, None]
    direct = [one, None, None, None]
    field = [None, None, None, None]
    rz = mu[0]
    for it in range(ITERS):
        moved = [None] + direct[:-1]
        alpha = rz / inner_product(direct, moved)
        field = [plus(a, alpha, b) for a, b in zip(field, direct)]
        resid = [plus(a, -alpha, b) for a, b in zip(resid, moved)]
        if it + 1 < ITERS:
            new = inner_product(resid, resid)
            beta = new / rz
            direct = [plus(a, beta, b) for a, b in zip(resid, direct)]
            rz = new
    out_field = field[0] * basis_ref[0]
    for i in range(1, ITERS):
        out_field = out_field + field[i] * basis_ref[i]
    out_resid = image_ref[0]
    for i in range(1, ITERS + 1):
        out_resid = out_resid + resid[i] * image_ref[i]
    field_ref[...] = out_field
    resid_ref[...] = out_resid
    for copy in first + in_flight:
        copy.wait_send()


def local(delta_flux, noise_var, pixel_pos, pixel_count, pair_list):
    slots = pair_list.shape[3]
    n_sky = lax.axis_size("sky")
    n_gz = lax.axis_size("gz")
    n_outer = n_sky // INNER
    pairs = pair_list[0, 0]
    vmem = pl.BlockSpec(memory_space=pltpu.VMEM)
    smem = pl.BlockSpec(memory_space=pltpu.SMEM)
    shape = jax.ShapeDtypeStruct((BLOCKS, WIDTH), f32)
    dma = pltpu.SemaphoreType.DMA
    field, resid = pl.pallas_call(
        functools.partial(body, slots),
        out_shape=(shape, shape),
        in_specs=[vmem, vmem, vmem, vmem, vmem, smem],
        out_specs=(vmem, vmem),
        scratch_shapes=[
            pltpu.VMEM((BLOCKS, WIDTH, WIDTH), bf16),
            pltpu.VMEM((slots + BLOCKS, 2 * WIDTH, WIDTH), bf16),
            pltpu.VMEM((4 * BLOCKS, WIDTH), f32),
            pltpu.VMEM((CODES, 4 * BLOCKS, WIDTH), f32),
            pltpu.VMEM((CODES, BLOCKS, WIDTH), f32),
            pltpu.VMEM((CODES, BLOCKS, WIDTH), f32),
            pltpu.VMEM((ITERS, CODES, 2 * BLOCKS, WIDTH), f32),
            pltpu.VMEM((ITERS, CODES, 2 * BLOCKS, WIDTH), f32),
            pltpu.VMEM((slots, WIDTH), f32),
            pltpu.VMEM((slots, WIDTH), f32),
            pltpu.VMEM((BLOCKS, WIDTH), f32),
            pltpu.VMEM((ITERS + 1, BLOCKS, WIDTH), f32),
            pltpu.VMEM((ITERS + 1, BLOCKS, WIDTH), f32),
            pltpu.VMEM((BLOCKS, 2 * slots), bf16),
            pltpu.VMEM((CODES * BLOCKS, 2 * slots), bf16),
            pltpu.VMEM((3, SUB, WIDTH), f32),
            pltpu.VMEM((n_gz - 1, SUB, WIDTH), f32),
            pltpu.VMEM((INNER - 1, SUB, WIDTH), f32),
            pltpu.VMEM((n_outer - 1, SUB, WIDTH), f32),
            dma((CODES,)), dma((CODES,)),
            dma((ITERS - 1, CODES)), dma((ITERS - 1, CODES)),
            dma((ITERS, CODES)), dma((ITERS, CODES)),
            dma((n_gz - 1,)), dma((n_gz - 1,)),
            dma((INNER - 1,)), dma((INNER - 1,)),
            dma((n_outer - 1,)), dma((n_outer - 1,)),
        ],
        compiler_params=pltpu.CompilerParams(
            collective_id=0, has_side_effects=True, vmem_limit_bytes=40 * 1024 * 1024
        ),
    )(
        delta_flux[0, 0],
        noise_var[0, 0],
        pixel_pos.reshape(3 * BLOCKS, WIDTH),
        pixel_count.reshape(1, BLOCKS),
        pairs,
        pairs,
    )
    return field[None, None], resid[None, None]


def solution(mesh):
    placed = (
        P("sky", "gz", None, None),
        P("sky", "gz", None, None),
        P("sky", "gz", None, None, None),
        P("sky", "gz", None),
        P("sky", "gz", None, None),
    )
    return jax.shard_map(
        local,
        mesh=mesh,
        in_specs=placed,
        out_specs=(P("sky", "gz", None, None), P("sky", "gz", None, None)),
        check_vma=False,
    )
```

```python
import functools
import math
import jax
import jax.numpy as jnp
from jax import lax
from jax.experimental import pallas as pl
from jax.experimental.pallas import tpu as pltpu
from jax.sharding import PartitionSpec as P

ITERS = 3
BLOCKS = 32
WIDTH = 128
CODES = 9
OWN = 4
SUB = 8
INNER = 8

signal_amp = 0.25
bf16 = jnp.bfloat16
f32 = jnp.float32


def mm(left, right):
    return lax.dot_general(left, right, (((1,), (0,)), ((), ())), preferred_element_type=f32)


def mm_trans(left, right):
    return lax.dot_general(left, right, (((1,), (1,)), ((), ())), preferred_element_type=f32)


def split_two(values):
    high = values.astype(bf16)
    return high, (values - high.astype(f32)).astype(bf16)


def split_three(values):
    high = values.astype(bf16).astype(f32)
    rest = values - high
    mid = rest.astype(bf16).astype(f32)
    return high, mid, rest - mid


def body(
    slots,
    delta_in, noise_in, pos_in, count_in, pair_in,
    field_ref, resid_ref,
    delta_ref, noise_ref, pos_ref, count_ref, pair_ref, spair_ref,
    near_ref, cov_ref, first_ref, halo0_ref, halo1_ref, halo2_ref, owed_ref, got_ref,
    gain_ref, pay_ref, self_ref, basis_ref, image_ref, onto_ref, from_ref,
    sum_ref, red1_ref, red2_ref, red3_ref,
    load_sem, first_send, first_recv, halo_send, halo_recv, owed_send, owed_recv,
    red1_send, red1_recv, red2_send, red2_recv, red3_send, red3_recv,
):
    n_sky = lax.axis_size("sky")
    n_gz = lax.axis_size("gz")
    n_outer = n_sky // INNER
    me_s = lax.axis_index("sky")
    me_g = lax.axis_index("gz")
    outer = me_s // INNER
    inner = me_s % INNER

    def tile_at(code):
        return (
            (me_s + code // 3 - 1 + n_sky) % n_sky,
            (me_g + code % 3 - 1 + n_gz) % n_gz,
        )

    def gz_at(step):
        return (me_s, (me_g + step) % n_gz)

    def inner_at(step):
        return (outer * INNER + (inner + step) % INNER, me_g)

    def outer_at(step):
        return ((outer + step) % n_outer * INNER + inner, me_g)

    sides = [code for code in range(CODES) if code != OWN]
    partners = [tile_at(code) for code in sides]
    partners += [gz_at(step) for step in range(1, n_gz)]
    partners += [inner_at(step) for step in range(1, INNER)]
    partners += [outer_at(step) for step in range(1, n_outer)]
    loads = [
        pltpu.make_async_copy(source, into, load_sem.at[i])
        for i, (source, into) in enumerate(
            (
                (pos_in.at[0, 0], pos_ref),
                (pair_in.at[0], pair_ref),
                (pair_in.at[0], spair_ref),
                (count_in.at[0], count_ref),
                (noise_in.at[0, 0], noise_ref),
                (delta_in.at[0, 0], delta_ref),
            )
        )
    ]
    for copy in loads:
        copy.start()
    barrier = pltpu.get_barrier_semaphore()
    for partner in partners:
        pl.semaphore_signal(
            barrier, inc=1, device_id=partner, device_id_type=pl.DeviceIdType.MESH
        )

    def remote(source, target, send, recv, device):
        return pltpu.make_async_remote_copy(
            src_ref=source, dst_ref=target, send_sem=send, recv_sem=recv,
            device_id=device, device_id_type=pl.DeviceIdType.MESH,
        )

    for copy in loads:
        copy.wait()
    pl.semaphore_wait(barrier, len(partners))
    first = [
        remote(pos_ref, first_ref.at[8 - c], first_send.at[c], first_recv.at[8 - c], tile_at(c))
        for c in sides
    ]
    for copy in first:
        copy.start()
    first_ref[OWN] = pos_ref[...]

    def halo_copies(it, into):
        return [
            remote(
                basis_ref.at[it], into.at[8 - c],
                halo_send.at[it, c], halo_recv.at[it, 8 - c], tile_at(c),
            )
            for c in sides
        ]

    eye_b = lax.broadcasted_iota(jnp.int32, (BLOCKS, BLOCKS), 0) == lax.broadcasted_iota(
        jnp.int32, (BLOCKS, BLOCKS), 1
    )
    count = jnp.sum(
        jnp.where(eye_b, count_ref[...].astype(f32), 0.0), axis=1, keepdims=True
    )
    lanes = lax.broadcasted_iota(jnp.int32, (BLOCKS, WIDTH), 1).astype(f32)
    live = (lanes < count).astype(f32)
    noise = noise_ref[...]
    precond = 1.0 / (noise + signal_amp)
    right_side = live * delta_ref[...]
    image_ref[0] = right_side
    basis_ref[0] = precond * right_side

    halo_refs = (halo0_ref, halo1_ref, halo2_ref)
    arriving = halo_copies(0, halo0_ref)
    for copy in arriving:
        copy.start()
    halo0_ref[OWN] = basis_ref[0]

    codes = pair_ref[0]
    near_row = (codes >= 3).astype(jnp.int32) + (codes >= 6).astype(jnp.int32)
    row_s = me_s + near_row - 1
    row_g = me_g + (codes - 3 * near_row) - 1
    filled = codes < CODES
    inside = filled & (row_s >= 0) & (row_s < n_sky) & (row_g >= 0) & (row_g < n_gz)
    flat = jnp.minimum(codes, CODES - 1) * BLOCKS + pair_ref[1]
    target = pair_ref[2]
    weight = jnp.where(inside, signal_amp, 0.0)
    rows_b = lax.broadcasted_iota(jnp.int32, (BLOCKS, slots), 0)
    hits = rows_b == target
    onto = jnp.where(hits, weight, 0.0)
    onto_ref[:, :slots] = onto.astype(bf16)
    onto_ref[:, slots:] = onto.astype(bf16)
    named = jnp.sum(
        jnp.where(hits & filled, signal_amp, 0.0), axis=1, keepdims=True
    )
    rows_f = lax.broadcasted_iota(jnp.int32, (CODES * BLOCKS, slots), 0)
    backs = jnp.where(rows_f == flat, weight, 0.0)
    from_ref[:, :slots] = backs.astype(bf16)
    from_ref[:, slots:] = backs.astype(bf16)
    sourced = jnp.broadcast_to(
        jnp.sum(backs, axis=1, keepdims=True), (CODES * BLOCKS, WIDTH)
    )
    for c in range(CODES):
        owed_ref[0, c, BLOCKS:] = sourced[c * BLOCKS : (c + 1) * BLOCKS]

    mid_x = (2 * me_s + 1).astype(f32)
    mid_z = (4 * me_g + 2).astype(f32)
    scale = math.sqrt(math.log2(math.e))
    sub = lax.broadcasted_iota(jnp.int32, (SUB, WIDTH), 0)

    def features(code, block, swap):
        x = (first_ref[code, 0, pl.ds(block, 1), :] - mid_x) * scale
        y = (first_ref[code, 1, pl.ds(block, 1), :] - 1.0) * scale
        z = (first_ref[code, 2, pl.ds(block, 1), :] - mid_z) * scale
        size = -0.5 * (x * x + y * y + z * z)
        tile = jnp.where(sub == 0, x, 0.0)
        tile = jnp.where(sub == 1, y, tile)
        tile = jnp.where(sub == 2, z, tile)
        tile = jnp.where(sub == (3 if swap else 4), size, tile)
        return jnp.where(sub == (4 if swap else 3), 1.0, tile)

    blank = jnp.zeros((WIDTH - 6 * SUB, WIDTH), f32)

    def near_step(block, _):
        h, m, l = split_three(features(OWN, block, True))
        stack = jnp.concatenate([h, h, m, m, h, l, blank], axis=0)
        near_ref[block] = jnp.transpose(stack).astype(bf16)
        return 0

    lax.fori_loop(0, BLOCKS, near_step, 0)

    def make_tile(slot, block, code, source):
        h, m, l = split_three(features(code, source, False))
        stack = jnp.concatenate([h, m, h, m, l, h, blank], axis=0).astype(bf16)
        values = jnp.exp2(mm(near_ref[block], stack))
        high, low = split_two(values)
        cov_ref[slot, 0:WIDTH] = high
        cov_ref[slot, WIDTH:] = low

    def self_tile(step, _):
        for k in range(4):
            block = step * 4 + k
            make_tile(slots + block, block, OWN, block)
        return 0

    lax.fori_loop(0, BLOCKS // 4, self_tile, 0)
    for copy in first:
        copy.wait_recv()

    def packed(rows):
        high, low = split_two(rows)
        return jnp.concatenate([high, low], axis=0)

    def doubled(values):
        high, low = split_two(values)
        return jnp.concatenate([high, low], axis=0)

    in_flight = []
    own_weight = None
    for it in range(ITERS):
        vector = basis_ref[it]
        halo_ref = halo_refs[it]
        if it > 0:
            arriving = halo_copies(it, halo_ref)
            for copy in arriving:
                copy.start()
            halo_ref[OWN] = vector

        def pay_step(step, _):
            if it == 0:
                for k in range(SUB):
                    slot = step * SUB + k
                    code = jnp.minimum(spair_ref[0, 0, slot], CODES - 1)
                    make_tile(slot, spair_ref[2, 0, slot], code, spair_ref[1, 0, slot])
            rows = jnp.zeros((SUB, WIDTH), f32)
            for k in range(SUB):
                block = spair_ref[2, 0, step * SUB + k]
                rows = jnp.where(sub == k, basis_ref[it, pl.ds(block, 1), :], rows)
            left = packed(rows)
            left = jnp.concatenate([left, left], axis=1)
            total = jnp.zeros((SUB, WIDTH), f32)
            for k in range(SUB):
                out = mm(left, cov_ref[step * SUB + k])
                total = jnp.where(sub == k, out[:SUB] + out[SUB:], total)
            pay_ref[pl.ds(step * SUB, SUB), :] = total
            return 0

        lax.fori_loop(0, slots // SUB, pay_step, 0)
        owed = mm(from_ref[...], doubled(pay_ref[...]))
        for c in range(CODES):
            owed_ref[it, c, 0:BLOCKS] = owed[c * BLOCKS : (c + 1) * BLOCKS]
        extent = 2 * BLOCKS if it == 0 else BLOCKS
        returns = [
            remote(
                owed_ref.at[it, c, pl.ds(0, extent)], got_ref.at[it, 8 - c, pl.ds(0, extent)],
                owed_send.at[it, c], owed_recv.at[it, 8 - c], tile_at(c),
            )
            for c in sides
        ]
        for copy in returns:
            copy.start()

        def self_step(step, _):
            left = packed(basis_ref[it, pl.ds(step * SUB, SUB), :])
            left = jnp.concatenate([left, left], axis=1)
            total = jnp.zeros((SUB, WIDTH), f32)
            for k in range(SUB):
                out = mm(left, cov_ref[slots + step * SUB + k])
                total = jnp.where(sub == k, out[:SUB] + out[SUB:], total)
            self_ref[pl.ds(step * SUB, SUB), :] = total
            return 0

        lax.fori_loop(0, BLOCKS // SUB, self_step, 0)
        for copy in arriving:
            copy.wait_recv()

        def gain_step(step, _):
            rows = jnp.zeros((SUB, WIDTH), f32)
            for k in range(SUB):
                slot = step * SUB + k
                code = jnp.minimum(spair_ref[0, 0, slot], CODES - 1)
                rows = jnp.where(sub == k, halo_ref[code, pl.ds(spair_ref[1, 0, slot], 1), :], rows)
            left = packed(rows)
            total = jnp.zeros((SUB, WIDTH), f32)
            for k in range(SUB):
                out = mm_trans(left, cov_ref[step * SUB + k])
                out = out[:SUB] + out[SUB:]
                total = jnp.where(sub == k, out[:, :WIDTH] + out[:, WIDTH:], total)
            gain_ref[pl.ds(step * SUB, SUB), :] = total
            return 0

        lax.fori_loop(0, slots // SUB, gain_step, 0)
        totals = mm(onto_ref[...], doubled(gain_ref[...])) + owed_ref[it, OWN, 0:BLOCKS]
        for copy in returns:
            copy.wait_recv()
        for c in sides:
            totals = totals + got_ref[it, c, 0:BLOCKS]
        if it == 0:
            own_weight = owed_ref[0, OWN, BLOCKS:] + (signal_amp + named)
            for c in sides:
                own_weight = own_weight + got_ref[0, c, BLOCKS:]
        totals = totals + own_weight * self_ref[...]
        image = live * totals + noise * vector
        image_ref[it + 1] = image
        basis_ref[it + 1] = precond * image
        in_flight += arriving + returns

    moments = jnp.zeros((SUB, WIDTH), f32)
    for m in range(2 * ITERS + 1):
        product = basis_ref[m // 2] * image_ref[m - m // 2]
        moments = jnp.where(sub == m, jnp.sum(product, axis=0, keepdims=True), moments)
    stages = (
        (gz_at, n_gz, red1_ref, red1_send, red1_recv),
        (inner_at, INNER, red2_ref, red2_send, red2_recv),
        (outer_at, n_outer, red3_ref, red3_send, red3_recv),
    )
    for stage, (device_at, members, into, send, recv) in enumerate(stages):
        sum_ref[stage] = moments
        copies = [
            remote(
                sum_ref.at[stage], into.at[step - 1], send.at[step - 1], recv.at[step - 1],
                device_at(step),
            )
            for step in range(1, members)
        ]
        for copy in copies:
            copy.start()
        for step, copy in enumerate(copies):
            copy.wait_recv()
            moments = moments + into[step]
        in_flight += copies
    total = jnp.sum(moments, axis=1, keepdims=True)
    mu = [total[m : m + 1] for m in range(2 * ITERS + 1)]

    def inner_product(left, right):
        value = None
        for i, a in enumerate(left):
            for j, b in enumerate(right):
                if a is not None and b is not None:
                    term = a * b * mu[i + j]
                    value = term if value is None else value + term
        return value

    def plus(left, scale, right):
        if right is None:
            return left
        return scale * right if left is None else left + scale * right

    one = jnp.ones((1, 1), f32)
    resid = [one, None, None, None]
    direct = [one, None, None, None]
    field = [None, None, None, None]
    rz = mu[0]
    for it in range(ITERS):
        moved = [None] + direct[:-1]
        alpha = rz / inner_product(direct, moved)
        field = [plus(a, alpha, b) for a, b in zip(field, direct)]
        resid = [plus(a, -alpha, b) for a, b in zip(resid, moved)]
        if it + 1 < ITERS:
            new = inner_product(resid, resid)
            beta = new / rz
            direct = [plus(a, beta, b) for a, b in zip(resid, direct)]
            rz = new
    out_field = field[0] * basis_ref[0]
    for i in range(1, ITERS):
        out_field = out_field + field[i] * basis_ref[i]
    out_resid = image_ref[0]
    for i in range(1, ITERS + 1):
        out_resid = out_resid + resid[i] * image_ref[i]
    field_ref[...] = out_field
    resid_ref[...] = out_resid
    for copy in first + in_flight:
        copy.wait_send()


def local(delta_flux, noise_var, pixel_pos, pixel_count, pair_list):
    slots = pair_list.shape[3]
    n_sky = lax.axis_size("sky")
    n_gz = lax.axis_size("gz")
    n_outer = n_sky // INNER
    vmem = pl.BlockSpec(memory_space=pltpu.VMEM)
    hbm = pl.BlockSpec(memory_space=pltpu.HBM)
    shape = jax.ShapeDtypeStruct((BLOCKS, WIDTH), f32)
    dma = pltpu.SemaphoreType.DMA
    field, resid = pl.pallas_call(
        functools.partial(body, slots),
        out_shape=(shape, shape),
        in_specs=[hbm] * 5,
        out_specs=(vmem, vmem),
        scratch_shapes=[
            pltpu.VMEM((BLOCKS, WIDTH), f32),
            pltpu.VMEM((BLOCKS, WIDTH), f32),
            pltpu.VMEM((3, BLOCKS, WIDTH), f32),
            pltpu.VMEM((1, BLOCKS), jnp.int32),
            pltpu.VMEM((3, 1, slots), jnp.int32),
            pltpu.SMEM((3, 1, slots), jnp.int32),
            pltpu.VMEM((BLOCKS, WIDTH, WIDTH), bf16),
            pltpu.VMEM((slots + BLOCKS, 2 * WIDTH, WIDTH), bf16),
            pltpu.VMEM((CODES, 3, BLOCKS, WIDTH), f32),
            pltpu.VMEM((CODES, BLOCKS, WIDTH), f32),
            pltpu.VMEM((CODES, BLOCKS, WIDTH), f32),
            pltpu.VMEM((CODES, BLOCKS, WIDTH), f32),
            pltpu.VMEM((ITERS, CODES, 2 * BLOCKS, WIDTH), f32),
            pltpu.VMEM((ITERS, CODES, 2 * BLOCKS, WIDTH), f32),
            pltpu.VMEM((slots, WIDTH), f32),
            pltpu.VMEM((slots, WIDTH), f32),
            pltpu.VMEM((BLOCKS, WIDTH), f32),
            pltpu.VMEM((ITERS + 1, BLOCKS, WIDTH), f32),
            pltpu.VMEM((ITERS + 1, BLOCKS, WIDTH), f32),
            pltpu.VMEM((BLOCKS, 2 * slots), bf16),
            pltpu.VMEM((CODES * BLOCKS, 2 * slots), bf16),
            pltpu.VMEM((3, SUB, WIDTH), f32),
            pltpu.VMEM((n_gz - 1, SUB, WIDTH), f32),
            pltpu.VMEM((INNER - 1, SUB, WIDTH), f32),
            pltpu.VMEM((n_outer - 1, SUB, WIDTH), f32),
            dma((6,)), dma((CODES,)), dma((CODES,)),
            dma((ITERS, CODES)), dma((ITERS, CODES)),
            dma((ITERS, CODES)), dma((ITERS, CODES)),
            dma((n_gz - 1,)), dma((n_gz - 1,)),
            dma((INNER - 1,)), dma((INNER - 1,)),
            dma((n_outer - 1,)), dma((n_outer - 1,)),
        ],
        compiler_params=pltpu.CompilerParams(
            collective_id=0, has_side_effects=True, vmem_limit_bytes=40 * 1024 * 1024
        ),
    )(
        *(
            pltpu.with_memory_space_constraint(value, pltpu.HBM)
            for value in (
                delta_flux, noise_var, pixel_pos, pixel_count, jnp.transpose(pair_list, (0, 2, 1, 3))
            )
        )
    )
    return field[None, None], resid[None, None]


def solution(mesh):
    placed = (
        P("sky", "gz", None, None),
        P("sky", "gz", None, None),
        P("sky", "gz", None, None, None),
        P("sky", "gz", None),
        P("sky", "gz", None, None),
    )
    return jax.shard_map(
        local,
        mesh=mesh,
        in_specs=placed,
        out_specs=(P("sky", "gz", None, None), P("sky", "gz", None, None)),
        check_vma=False,
    )
```

```python
import functools
import math
import jax
import jax.numpy as jnp
from jax import lax
from jax.experimental import pallas as pl
from jax.experimental.pallas import tpu as pltpu
from jax.sharding import PartitionSpec as P

ITERS = 3
BLOCKS = 32
WIDTH = 128
CODES = 9
OWN = 4
SUB = 8
INNER = 8
BY_UNIT = (1, 4, 7)

signal_amp = 0.25
bf16 = jnp.bfloat16
f32 = jnp.float32


def mm(left, right):
    return lax.dot_general(left, right, (((1,), (0,)), ((), ())), preferred_element_type=f32)


def mm_trans(left, right):
    return lax.dot_general(left, right, (((1,), (1,)), ((), ())), preferred_element_type=f32)


def split_two(values):
    high = values.astype(bf16)
    return high, (values - high.astype(f32)).astype(bf16)


def split_three(values):
    high = values.astype(bf16).astype(f32)
    rest = values - high
    mid = rest.astype(bf16).astype(f32)
    return high, mid, rest - mid


def body(
    slots,
    delta_in, noise_in, pos_in, count_in, pair_in,
    field_ref, resid_ref,
    delta_ref, noise_ref, pos_ref, count_ref, pair_ref, spair_ref,
    near_ref, cov_ref, column_ref, first_ref, halo0_ref, halo1_ref, halo2_ref, owed_ref, got_ref,
    pay_ref, self_ref, basis_ref, image_ref, onto_ref, from_ref,
    sum_ref, red1_ref, red2_ref, red3_ref,
    load_sem, first_send, first_recv, halo_send, halo_recv, owed_send, owed_recv,
    red1_send, red1_recv, red2_send, red2_recv, red3_send, red3_recv,
):
    n_sky = lax.axis_size("sky")
    n_gz = lax.axis_size("gz")
    n_outer = n_sky // INNER
    me_s = lax.axis_index("sky")
    me_g = lax.axis_index("gz")
    outer = me_s // INNER
    inner = me_s % INNER

    def tile_at(code):
        return (
            (me_s + code // 3 - 1 + n_sky) % n_sky,
            (me_g + code % 3 - 1 + n_gz) % n_gz,
        )

    def gz_at(step):
        return (me_s, (me_g + step) % n_gz)

    def inner_at(step):
        return (outer * INNER + (inner + step) % INNER, me_g)

    def outer_at(step):
        return ((outer + step) % n_outer * INNER + inner, me_g)

    sides = [code for code in range(CODES) if code != OWN]
    partners = [tile_at(code) for code in sides]
    partners += [gz_at(step) for step in range(1, n_gz)]
    partners += [inner_at(step) for step in range(1, INNER)]
    partners += [outer_at(step) for step in range(1, n_outer)]
    loads = [
        pltpu.make_async_copy(source, into, load_sem.at[i])
        for i, (source, into) in enumerate(
            (
                (pos_in.at[0, 0], pos_ref),
                (pair_in.at[0], pair_ref),
                (pair_in.at[0], spair_ref),
                (count_in.at[0], count_ref),
                (noise_in.at[0, 0], noise_ref),
                (delta_in.at[0, 0], delta_ref),
            )
        )
    ]
    for copy in loads:
        copy.start()
    barrier = pltpu.get_barrier_semaphore()
    for partner in partners:
        pl.semaphore_signal(
            barrier, inc=1, device_id=partner, device_id_type=pl.DeviceIdType.MESH
        )

    def remote(source, target, send, recv, device):
        return pltpu.make_async_remote_copy(
            src_ref=source, dst_ref=target, send_sem=send, recv_sem=recv,
            device_id=device, device_id_type=pl.DeviceIdType.MESH,
        )

    for copy in loads:
        copy.wait()
    pl.semaphore_wait(barrier, len(partners))
    first = [
        remote(pos_ref, first_ref.at[8 - c], first_send.at[c], first_recv.at[8 - c], tile_at(c))
        for c in sides
    ]
    for copy in first:
        copy.start()
    first_ref[OWN] = pos_ref[...]

    def halo_copies(it, into):
        return [
            remote(
                basis_ref.at[it], into.at[8 - c],
                halo_send.at[it, c], halo_recv.at[it, 8 - c], tile_at(c),
            )
            for c in sides
        ]

    eye_b = lax.broadcasted_iota(jnp.int32, (BLOCKS, BLOCKS), 0) == lax.broadcasted_iota(
        jnp.int32, (BLOCKS, BLOCKS), 1
    )
    count = jnp.sum(
        jnp.where(eye_b, count_ref[...].astype(f32), 0.0), axis=1, keepdims=True
    )
    lanes = lax.broadcasted_iota(jnp.int32, (BLOCKS, WIDTH), 1).astype(f32)
    live = (lanes < count).astype(f32)
    noise = noise_ref[...]
    precond = 1.0 / (noise + signal_amp)
    right_side = live * delta_ref[...]
    image_ref[0] = right_side
    basis_ref[0] = precond * right_side

    halo_refs = (halo0_ref, halo1_ref, halo2_ref)
    arriving = halo_copies(0, halo0_ref)
    for copy in arriving:
        copy.start()
    halo0_ref[OWN] = basis_ref[0]

    codes = pair_ref[0]
    near_row = (codes >= 3).astype(jnp.int32) + (codes >= 6).astype(jnp.int32)
    row_s = me_s + near_row - 1
    row_g = me_g + (codes - 3 * near_row) - 1
    filled = codes < CODES
    inside = filled & (row_s >= 0) & (row_s < n_sky) & (row_g >= 0) & (row_g < n_gz)
    flat = jnp.minimum(codes, CODES - 1) * BLOCKS + pair_ref[1]
    target = pair_ref[2]
    weight = jnp.where(inside, signal_amp, 0.0)
    rows_b = lax.broadcasted_iota(jnp.int32, (BLOCKS, slots), 0)
    hits = rows_b == target
    onto = jnp.where(hits, weight, 0.0)
    onto_ref[:, :slots] = onto.astype(bf16)
    onto_ref[:, slots:] = onto.astype(bf16)
    named = jnp.sum(
        jnp.where(hits & filled, signal_amp, 0.0), axis=1, keepdims=True
    )
    rows_f = lax.broadcasted_iota(jnp.int32, (CODES * BLOCKS, slots), 0)
    backs = jnp.where(rows_f == flat, weight, 0.0)
    from_ref[:, :slots] = backs.astype(bf16)
    from_ref[:, slots:] = backs.astype(bf16)
    sourced = jnp.broadcast_to(
        jnp.sum(backs, axis=1, keepdims=True), (CODES * BLOCKS, WIDTH)
    )
    for c in range(CODES):
        owed_ref[0, c, BLOCKS:] = sourced[c * BLOCKS : (c + 1) * BLOCKS]

    mid_x = (2 * me_s + 1).astype(f32)
    mid_z = (4 * me_g + 2).astype(f32)
    scale = math.sqrt(math.log2(math.e))
    sub = lax.broadcasted_iota(jnp.int32, (SUB, WIDTH), 0)

    def features(code, block, swap):
        x = (first_ref[code, 0, pl.ds(block, 1), :] - mid_x) * scale
        y = (first_ref[code, 1, pl.ds(block, 1), :] - 1.0) * scale
        z = (first_ref[code, 2, pl.ds(block, 1), :] - mid_z) * scale
        size = -0.5 * (x * x + y * y + z * z)
        tile = jnp.where(sub == 0, x, 0.0)
        tile = jnp.where(sub == 1, y, tile)
        tile = jnp.where(sub == 2, z, tile)
        tile = jnp.where(sub == (3 if swap else 4), size, tile)
        return jnp.where(sub == (4 if swap else 3), 1.0, tile)

    blank = jnp.zeros((WIDTH - 6 * SUB, WIDTH), f32)

    def near_step(block, _):
        h, m, l = split_three(features(OWN, block, True))
        stack = jnp.concatenate([h, h, m, m, h, l, blank], axis=0)
        near_ref[block] = jnp.transpose(stack).astype(bf16)
        return 0

    lax.fori_loop(0, BLOCKS, near_step, 0)

    def make_tile(slot, block, code, source):
        h, m, l = split_three(features(code, source, False))
        stack = jnp.concatenate([h, m, h, m, l, h, blank], axis=0).astype(bf16)
        cov_ref[slot] = jnp.exp2(mm(near_ref[block], stack))

    def self_tile(step, _):
        for k in range(4):
            block = step * 4 + k
            make_tile(slots + block, block, OWN, block)
        return 0

    lax.fori_loop(0, BLOCKS // 4, self_tile, 0)
    for copy in first:
        copy.wait_recv()

    def spread(values):
        tall = jnp.transpose(
            jnp.concatenate([values, jnp.zeros((WIDTH - BLOCKS, WIDTH), f32)], axis=0)
        )
        for block in range(BLOCKS):
            column_ref[block] = jnp.broadcast_to(tall[:, block : block + 1], (WIDTH, WIDTH))

    def down(slot, block):
        product = cov_ref[slot] * column_ref[block]
        return jnp.sum(
            jnp.sum(product.reshape(WIDTH // SUB, SUB, WIDTH), axis=0), axis=0, keepdims=True
        )

    def doubled(values):
        high, low = split_two(values)
        return jnp.concatenate([high, low], axis=0)

    lanes_sq = lax.broadcasted_iota(jnp.int32, (WIDTH, slots), 1)
    ones = jnp.ones((2 * WIDTH, WIDTH), bf16)
    in_flight = []
    own_weight = None
    for it in range(ITERS):
        vector = basis_ref[it]
        halo_ref = halo_refs[it]
        if it > 0:
            arriving = halo_copies(it, halo_ref)
            for copy in arriving:
                copy.start()
            halo_ref[OWN] = vector

        spread(vector)

        def pay_step(step, _):
            if it == 0:
                for k in range(SUB):
                    slot = step * SUB + k
                    code = jnp.minimum(spair_ref[0, 0, slot], CODES - 1)
                    make_tile(slot, spair_ref[2, 0, slot], code, spair_ref[1, 0, slot])
            total = jnp.zeros((SUB, WIDTH), f32)
            for k in range(SUB):
                slot = step * SUB + k
                total = jnp.where(sub == k, down(slot, spair_ref[2, 0, slot]), total)
            pay_ref[pl.ds(step * SUB, SUB), :] = total
            return 0

        lax.fori_loop(0, slots // SUB, pay_step, 0)
        owed = mm(from_ref[...], doubled(pay_ref[...]))
        for c in range(CODES):
            owed_ref[it, c, 0:BLOCKS] = owed[c * BLOCKS : (c + 1) * BLOCKS]
        extent = 2 * BLOCKS if it == 0 else BLOCKS
        returns = [
            remote(
                owed_ref.at[it, c, pl.ds(0, extent)], got_ref.at[it, 8 - c, pl.ds(0, extent)],
                owed_send.at[it, c], owed_recv.at[it, 8 - c], tile_at(c),
            )
            for c in sides
        ]
        for copy in returns:
            copy.start()

        def self_step(step, _):
            total = jnp.zeros((SUB, WIDTH), f32)
            for k in range(SUB):
                block = step * SUB + k
                total = jnp.where(sub == k, down(slots + block, block), total)
            self_ref[pl.ds(step * SUB, SUB), :] = total
            return 0

        lax.fori_loop(0, BLOCKS // SUB, self_step, 0)
        for copy in arriving:
            copy.wait_recv()

        def gain_step(step, tall):
            for k in range(SUB):
                slot = step * SUB + k
                code = jnp.minimum(spair_ref[0, 0, slot], CODES - 1)
                row = halo_ref[code, pl.ds(spair_ref[1, 0, slot], 1), :]
                product = cov_ref[slot] * row
                if k in BY_UNIT:
                    high, low = split_two(product)
                    reach = mm(jnp.concatenate([high, low], axis=1), ones)
                else:
                    reach = jnp.sum(product, axis=1, keepdims=True)
                tall = jnp.where(lanes_sq == slot, reach, tall)
            return tall

        tall = lax.fori_loop(0, slots // SUB, gain_step, jnp.zeros((WIDTH, slots), f32))
        high, low = split_two(tall)
        totals = mm_trans(onto_ref[...], jnp.concatenate([high, low], axis=1))
        totals = totals + owed_ref[it, OWN, 0:BLOCKS]
        for copy in returns:
            copy.wait_recv()
        for c in sides:
            totals = totals + got_ref[it, c, 0:BLOCKS]
        if it == 0:
            own_weight = owed_ref[0, OWN, BLOCKS:] + (signal_amp + named)
            for c in sides:
                own_weight = own_weight + got_ref[0, c, BLOCKS:]
        totals = totals + own_weight * self_ref[...]
        image = live * totals + noise * vector
        image_ref[it + 1] = image
        basis_ref[it + 1] = precond * image
        in_flight += arriving + returns

    moments = jnp.zeros((SUB, WIDTH), f32)
    for m in range(2 * ITERS + 1):
        product = basis_ref[m // 2] * image_ref[m - m // 2]
        moments = jnp.where(sub == m, jnp.sum(product, axis=0, keepdims=True), moments)
    stages = (
        (gz_at, n_gz, red1_ref, red1_send, red1_recv),
        (inner_at, INNER, red2_ref, red2_send, red2_recv),
        (outer_at, n_outer, red3_ref, red3_send, red3_recv),
    )
    for stage, (device_at, members, into, send, recv) in enumerate(stages):
        sum_ref[stage] = moments
        copies = [
            remote(
                sum_ref.at[stage], into.at[step - 1], send.at[step - 1], recv.at[step - 1],
                device_at(step),
            )
            for step in range(1, members)
        ]
        for copy in copies:
            copy.start()
        for step, copy in enumerate(copies):
            copy.wait_recv()
            moments = moments + into[step]
        in_flight += copies
    total = jnp.sum(moments, axis=1, keepdims=True)
    mu = [total[m : m + 1] for m in range(2 * ITERS + 1)]

    def inner_product(left, right):
        value = None
        for i, a in enumerate(left):
            for j, b in enumerate(right):
                if a is not None and b is not None:
                    term = a * b * mu[i + j]
                    value = term if value is None else value + term
        return value

    def plus(left, scale, right):
        if right is None:
            return left
        return scale * right if left is None else left + scale * right

    one = jnp.ones((1, 1), f32)
    resid = [one, None, None, None]
    direct = [one, None, None, None]
    field = [None, None, None, None]
    rz = mu[0]
    for it in range(ITERS):
        moved = [None] + direct[:-1]
        alpha = rz / inner_product(direct, moved)
        field = [plus(a, alpha, b) for a, b in zip(field, direct)]
        resid = [plus(a, -alpha, b) for a, b in zip(resid, moved)]
        if it + 1 < ITERS:
            new = inner_product(resid, resid)
            beta = new / rz
            direct = [plus(a, beta, b) for a, b in zip(resid, direct)]
            rz = new
    out_field = field[0] * basis_ref[0]
    for i in range(1, ITERS):
        out_field = out_field + field[i] * basis_ref[i]
    out_resid = image_ref[0]
    for i in range(1, ITERS + 1):
        out_resid = out_resid + resid[i] * image_ref[i]
    field_ref[...] = out_field
    resid_ref[...] = out_resid
    for copy in first + in_flight:
        copy.wait_send()


def local(delta_flux, noise_var, pixel_pos, pixel_count, pair_list):
    slots = pair_list.shape[3]
    n_sky = lax.axis_size("sky")
    n_gz = lax.axis_size("gz")
    n_outer = n_sky // INNER
    vmem = pl.BlockSpec(memory_space=pltpu.VMEM)
    hbm = pl.BlockSpec(memory_space=pltpu.HBM)
    shape = jax.ShapeDtypeStruct((BLOCKS, WIDTH), f32)
    dma = pltpu.SemaphoreType.DMA
    field, resid = pl.pallas_call(
        functools.partial(body, slots),
        out_shape=(shape, shape),
        in_specs=[hbm] * 5,
        out_specs=(vmem, vmem),
        scratch_shapes=[
            pltpu.VMEM((BLOCKS, WIDTH), f32),
            pltpu.VMEM((BLOCKS, WIDTH), f32),
            pltpu.VMEM((3, BLOCKS, WIDTH), f32),
            pltpu.VMEM((1, BLOCKS), jnp.int32),
            pltpu.VMEM((3, 1, slots), jnp.int32),
            pltpu.SMEM((3, 1, slots), jnp.int32),
            pltpu.VMEM((BLOCKS, WIDTH, WIDTH), bf16),
            pltpu.VMEM((slots + BLOCKS, WIDTH, WIDTH), f32),
            pltpu.VMEM((BLOCKS, WIDTH, WIDTH), f32),
            pltpu.VMEM((CODES, 3, BLOCKS, WIDTH), f32),
            pltpu.VMEM((CODES, BLOCKS, WIDTH), f32),
            pltpu.VMEM((CODES, BLOCKS, WIDTH), f32),
            pltpu.VMEM((CODES, BLOCKS, WIDTH), f32),
            pltpu.VMEM((ITERS, CODES, 2 * BLOCKS, WIDTH), f32),
            pltpu.VMEM((ITERS, CODES, 2 * BLOCKS, WIDTH), f32),
            pltpu.VMEM((slots, WIDTH), f32),
            pltpu.VMEM((BLOCKS, WIDTH), f32),
            pltpu.VMEM((ITERS + 1, BLOCKS, WIDTH), f32),
            pltpu.VMEM((ITERS + 1, BLOCKS, WIDTH), f32),
            pltpu.VMEM((BLOCKS, 2 * slots), bf16),
            pltpu.VMEM((CODES * BLOCKS, 2 * slots), bf16),
            pltpu.VMEM((3, SUB, WIDTH), f32),
            pltpu.VMEM((n_gz - 1, SUB, WIDTH), f32),
            pltpu.VMEM((INNER - 1, SUB, WIDTH), f32),
            pltpu.VMEM((n_outer - 1, SUB, WIDTH), f32),
            dma((6,)), dma((CODES,)), dma((CODES,)),
            dma((ITERS, CODES)), dma((ITERS, CODES)),
            dma((ITERS, CODES)), dma((ITERS, CODES)),
            dma((n_gz - 1,)), dma((n_gz - 1,)),
            dma((INNER - 1,)), dma((INNER - 1,)),
            dma((n_outer - 1,)), dma((n_outer - 1,)),
        ],
        compiler_params=pltpu.CompilerParams(
            collective_id=0, has_side_effects=True, vmem_limit_bytes=40 * 1024 * 1024
        ),
    )(
        *(
            pltpu.with_memory_space_constraint(value, pltpu.HBM)
            for value in (
                delta_flux, noise_var, pixel_pos, pixel_count, jnp.transpose(pair_list, (0, 2, 1, 3))
            )
        )
    )
    return field[None, None], resid[None, None]


def solution(mesh):
    placed = (
        P("sky", "gz", None, None),
        P("sky", "gz", None, None),
        P("sky", "gz", None, None, None),
        P("sky", "gz", None),
        P("sky", "gz", None, None),
    )
    return jax.shard_map(
        local,
        mesh=mesh,
        in_specs=placed,
        out_specs=(P("sky", "gz", None, None), P("sky", "gz", None, None)),
        check_vma=False,
    )
```

```python
import functools
import math
import jax
import jax.numpy as jnp
from jax import lax
from jax.experimental import pallas as pl
from jax.experimental.pallas import tpu as pltpu
from jax.sharding import PartitionSpec as P

ITERS = 3
BLOCKS = 32
WIDTH = 128
CODES = 9
OWN = 4
SUB = 8
INNER = 8

signal_amp = 0.25
bf16 = jnp.bfloat16
f32 = jnp.float32


def mm(left, right):
    return lax.dot_general(left, right, (((1,), (0,)), ((), ())), preferred_element_type=f32)


def mm_trans(left, right):
    return lax.dot_general(left, right, (((1,), (1,)), ((), ())), preferred_element_type=f32)


def split_two(values):
    high = values.astype(bf16)
    return high, (values - high.astype(f32)).astype(bf16)


def split_three(values):
    high = values.astype(bf16).astype(f32)
    rest = values - high
    mid = rest.astype(bf16).astype(f32)
    return high, mid, rest - mid


def body(
    slots,
    delta_in, noise_in, pos_in, count_in, pair_in,
    field_ref, resid_ref,
    delta_ref, noise_ref, pos_ref, count_ref, pair_ref, order_ref, spair_ref,
    near_ref, cov_ref, running_ref, column_ref, first_ref, halo0_ref, halo1_ref, halo2_ref, owed_ref, got_ref,
    pay_ref, self_ref, basis_ref, image_ref, from_ref,
    sum_ref, red1_ref, red2_ref, red3_ref,
    load_sem, first_send, first_recv, halo_send, halo_recv, owed_send, owed_recv,
    red1_send, red1_recv, red2_send, red2_recv, red3_send, red3_recv,
):
    n_sky = lax.axis_size("sky")
    n_gz = lax.axis_size("gz")
    n_outer = n_sky // INNER
    me_s = lax.axis_index("sky")
    me_g = lax.axis_index("gz")
    outer = me_s // INNER
    inner = me_s % INNER

    def tile_at(code):
        return (
            (me_s + code // 3 - 1 + n_sky) % n_sky,
            (me_g + code % 3 - 1 + n_gz) % n_gz,
        )

    def gz_at(step):
        return (me_s, (me_g + step) % n_gz)

    def inner_at(step):
        return (outer * INNER + (inner + step) % INNER, me_g)

    def outer_at(step):
        return ((outer + step) % n_outer * INNER + inner, me_g)

    sides = [code for code in range(CODES) if code != OWN]
    partners = [tile_at(code) for code in sides]
    partners += [gz_at(step) for step in range(1, n_gz)]
    partners += [inner_at(step) for step in range(1, INNER)]
    partners += [outer_at(step) for step in range(1, n_outer)]
    loads = [
        pltpu.make_async_copy(source, into, load_sem.at[i])
        for i, (source, into) in enumerate(
            (
                (pos_in.at[0, 0], pos_ref),
                (pair_in.at[0], pair_ref),
                (count_in.at[0], count_ref),
                (noise_in.at[0, 0], noise_ref),
                (delta_in.at[0, 0], delta_ref),
            )
        )
    ]
    for copy in loads:
        copy.start()
    barrier = pltpu.get_barrier_semaphore()
    for partner in partners:
        pl.semaphore_signal(
            barrier, inc=1, device_id=partner, device_id_type=pl.DeviceIdType.MESH
        )

    def remote(source, target, send, recv, device):
        return pltpu.make_async_remote_copy(
            src_ref=source, dst_ref=target, send_sem=send, recv_sem=recv,
            device_id=device, device_id_type=pl.DeviceIdType.MESH,
        )

    for copy in loads:
        copy.wait()
    pl.semaphore_wait(barrier, len(partners))
    first = [
        remote(pos_ref, first_ref.at[8 - c], first_send.at[c], first_recv.at[8 - c], tile_at(c))
        for c in sides
    ]
    for copy in first:
        copy.start()
    first_ref[OWN] = pos_ref[...]

    def halo_copies(it, into):
        return [
            remote(
                basis_ref.at[it], into.at[8 - c],
                halo_send.at[it, c], halo_recv.at[it, 8 - c], tile_at(c),
            )
            for c in sides
        ]

    eye_b = lax.broadcasted_iota(jnp.int32, (BLOCKS, BLOCKS), 0) == lax.broadcasted_iota(
        jnp.int32, (BLOCKS, BLOCKS), 1
    )
    count = jnp.sum(
        jnp.where(eye_b, count_ref[...].astype(f32), 0.0), axis=1, keepdims=True
    )
    lanes = lax.broadcasted_iota(jnp.int32, (BLOCKS, WIDTH), 1).astype(f32)
    live = (lanes < count).astype(f32)
    noise = noise_ref[...]
    precond = 1.0 / (noise + signal_amp)
    right_side = live * delta_ref[...]
    image_ref[0] = right_side
    basis_ref[0] = precond * right_side

    halo_refs = (halo0_ref, halo1_ref, halo2_ref)
    arriving = halo_copies(0, halo0_ref)
    for copy in arriving:
        copy.start()
    halo0_ref[OWN] = basis_ref[0]

    shape = (slots, slots)
    rows_s = lax.broadcasted_iota(jnp.int32, shape, 0)
    lanes_s = lax.broadcasted_iota(jnp.int32, shape, 1)
    codes = pair_ref[0]
    near_row = (codes >= 3).astype(jnp.int32) + (codes >= 6).astype(jnp.int32)
    row_s = me_s + near_row - 1
    row_g = me_g + (codes - 3 * near_row) - 1
    filled = codes < CODES
    inside = filled & (row_s >= 0) & (row_s < n_sky) & (row_g >= 0) & (row_g < n_gz)
    target = pair_ref[2]
    target_col = jnp.sum(jnp.where(rows_s == lanes_s, target, 0), axis=1, keepdims=True)
    before = (target < target_col) | ((target == target_col) & (lanes_s < rows_s))
    rank = jnp.sum(before.astype(jnp.int32), axis=1, keepdims=True)
    place = rank == lanes_s
    fields = (jnp.minimum(codes, CODES - 1), pair_ref[1], target, inside.astype(jnp.int32))
    limits = (CODES - 1, BLOCKS - 1, BLOCKS - 1, 1)
    sub = lax.broadcasted_iota(jnp.int32, (SUB, slots), 0)
    table = jnp.zeros((SUB, slots), jnp.int32)
    for i, (field, limit) in enumerate(zip(fields, limits)):
        column = jnp.sum(jnp.where(rows_s == lanes_s, field, 0), axis=1, keepdims=True)
        moved = jnp.sum(jnp.where(place, column, 0), axis=0, keepdims=True)
        table = jnp.where(sub == i, jnp.clip(moved, 0, limit), table)
    ends = jnp.sum((target_col <= lanes_s).astype(jnp.int32), axis=0, keepdims=True)
    table = jnp.where(sub == len(fields), jnp.clip(ends, 0, slots), table)
    order_ref[...] = table
    to_scalar = pltpu.make_async_copy(order_ref, spair_ref, load_sem.at[5])
    to_scalar.start()

    flat = table[0:1] * BLOCKS + table[1:2]
    weight = table[3:4].astype(f32) * signal_amp
    hits = lax.broadcasted_iota(jnp.int32, (BLOCKS, slots), 0) == target
    named = jnp.sum(
        jnp.where(hits & filled, signal_amp, 0.0), axis=1, keepdims=True
    )
    rows_f = lax.broadcasted_iota(jnp.int32, (CODES * BLOCKS, slots), 0)
    backs = jnp.where(rows_f == flat, weight, 0.0)
    from_ref[:, :slots] = backs.astype(bf16)
    from_ref[:, slots:] = backs.astype(bf16)
    sourced = jnp.broadcast_to(
        jnp.sum(backs, axis=1, keepdims=True), (CODES * BLOCKS, WIDTH)
    )
    for c in range(CODES):
        owed_ref[0, c, BLOCKS:] = sourced[c * BLOCKS : (c + 1) * BLOCKS]

    mid_x = (2 * me_s + 1).astype(f32)
    mid_z = (4 * me_g + 2).astype(f32)
    scale = math.sqrt(math.log2(math.e))
    def features(code, block, swap):
        x = (first_ref[code, 0, pl.ds(block, 1), :] - mid_x) * scale
        y = (first_ref[code, 1, pl.ds(block, 1), :] - 1.0) * scale
        z = (first_ref[code, 2, pl.ds(block, 1), :] - mid_z) * scale
        size = -0.5 * (x * x + y * y + z * z)
        tile = jnp.where(sub == 0, x, 0.0)
        tile = jnp.where(sub == 1, y, tile)
        tile = jnp.where(sub == 2, z, tile)
        tile = jnp.where(sub == (3 if swap else 4), size, tile)
        return jnp.where(sub == (4 if swap else 3), 1.0, tile)

    blank = jnp.zeros((WIDTH - 6 * SUB, WIDTH), f32)

    def near_step(block, _):
        h, m, l = split_three(features(OWN, block, True))
        stack = jnp.concatenate([h, h, m, m, h, l, blank], axis=0)
        near_ref[block] = jnp.transpose(stack).astype(bf16)
        return 0

    lax.fori_loop(0, BLOCKS, near_step, 0)

    def make_tile(slot, block, code, source):
        h, m, l = split_three(features(code, source, False))
        stack = jnp.concatenate([h, m, h, m, l, h, blank], axis=0).astype(bf16)
        cov_ref[slot] = jnp.exp2(mm(near_ref[block], stack))

    def self_tile(step, _):
        for k in range(4):
            block = step * 4 + k
            make_tile(slots + block, block, OWN, block)
        return 0

    lax.fori_loop(0, BLOCKS // 4, self_tile, 0)
    to_scalar.wait()
    for copy in first:
        copy.wait_recv()

    def spread(values):
        for block in range(BLOCKS):
            column_ref[block] = jnp.transpose(
                jnp.broadcast_to(values[block : block + 1], (WIDTH, WIDTH))
            )

    def down(slot, block):
        product = cov_ref[slot] * column_ref[block]
        return jnp.sum(
            jnp.sum(product.reshape(WIDTH // SUB, SUB, WIDTH), axis=0), axis=0, keepdims=True
        )

    def doubled(values):
        high, low = split_two(values)
        return jnp.concatenate([high, low], axis=0)

    lanes_sq = lax.broadcasted_iota(jnp.int32, (WIDTH, WIDTH), 1)
    in_flight = []
    own_weight = None
    for it in range(ITERS):
        vector = basis_ref[it]
        halo_ref = halo_refs[it]
        if it > 0:
            arriving = halo_copies(it, halo_ref)
            for copy in arriving:
                copy.start()
            halo_ref[OWN] = vector

        spread(vector)

        def pay_step(step, _):
            if it == 0:
                for k in range(SUB):
                    slot = step * SUB + k
                    make_tile(slot, spair_ref[2, slot], spair_ref[0, slot], spair_ref[1, slot])
            total = jnp.zeros((SUB, WIDTH), f32)
            for k in range(SUB):
                slot = step * SUB + k
                total = jnp.where(sub == k, down(slot, spair_ref[2, slot]), total)
            pay_ref[pl.ds(step * SUB, SUB), :] = total
            return 0

        lax.fori_loop(0, slots // SUB, pay_step, 0)
        owed = mm(from_ref[...], doubled(pay_ref[...]))
        for c in range(CODES):
            owed_ref[it, c, 0:BLOCKS] = owed[c * BLOCKS : (c + 1) * BLOCKS]
        extent = 2 * BLOCKS if it == 0 else BLOCKS
        returns = [
            remote(
                owed_ref.at[it, c, pl.ds(0, extent)], got_ref.at[it, 8 - c, pl.ds(0, extent)],
                owed_send.at[it, c], owed_recv.at[it, 8 - c], tile_at(c),
            )
            for c in sides
        ]
        for copy in returns:
            copy.start()

        def self_step(step, _):
            total = jnp.zeros((SUB, WIDTH), f32)
            for k in range(SUB):
                block = step * SUB + k
                total = jnp.where(sub == k, down(slots + block, block), total)
            self_ref[pl.ds(step * SUB, SUB), :] = total
            return 0

        lax.fori_loop(0, BLOCKS // SUB, self_step, 0)
        for copy in arriving:
            copy.wait_recv()

        def gain_step(step, running):
            for k in range(SUB):
                slot = step * SUB + k
                row = halo_ref[spair_ref[0, slot], pl.ds(spair_ref[1, slot], 1), :]
                row = row * (spair_ref[3, slot].astype(f32) * signal_amp)
                same = spair_ref[2, slot] == spair_ref[2, jnp.maximum(slot - 1, 0)]
                running = running * same.astype(f32) + cov_ref[slot] * row
                running_ref[slot] = running
            return running

        lax.fori_loop(0, slots // SUB, gain_step, jnp.zeros((WIDTH, WIDTH), f32))
        tall = jnp.zeros((WIDTH, WIDTH), f32)
        for block in range(BLOCKS):
            end = spair_ref[4, block]
            start = spair_ref[4, block - 1] if block > 0 else 0
            reach = jnp.sum(running_ref[jnp.clip(end - 1, 0, slots - 1)], axis=1, keepdims=True)
            reach = reach * (end > start).astype(f32)
            tall = jnp.where(lanes_sq == block, reach, tall)
        totals = jnp.transpose(tall)[:BLOCKS]
        totals = totals + owed_ref[it, OWN, 0:BLOCKS]
        for copy in returns:
            copy.wait_recv()
        for c in sides:
            totals = totals + got_ref[it, c, 0:BLOCKS]
        if it == 0:
            own_weight = owed_ref[0, OWN, BLOCKS:] + (signal_amp + named)
            for c in sides:
                own_weight = own_weight + got_ref[0, c, BLOCKS:]
        totals = totals + own_weight * self_ref[...]
        image = live * totals + noise * vector
        image_ref[it + 1] = image
        basis_ref[it + 1] = precond * image
        in_flight += arriving + returns

    moments = jnp.zeros((SUB, WIDTH), f32)
    for m in range(2 * ITERS + 1):
        product = basis_ref[m // 2] * image_ref[m - m // 2]
        moments = jnp.where(sub == m, jnp.sum(product, axis=0, keepdims=True), moments)
    stages = (
        (gz_at, n_gz, red1_ref, red1_send, red1_recv),
        (inner_at, INNER, red2_ref, red2_send, red2_recv),
        (outer_at, n_outer, red3_ref, red3_send, red3_recv),
    )
    for stage, (device_at, members, into, send, recv) in enumerate(stages):
        sum_ref[stage] = moments
        copies = [
            remote(
                sum_ref.at[stage], into.at[step - 1], send.at[step - 1], recv.at[step - 1],
                device_at(step),
            )
            for step in range(1, members)
        ]
        for copy in copies:
            copy.start()
        for step, copy in enumerate(copies):
            copy.wait_recv()
            moments = moments + into[step]
        in_flight += copies
    total = jnp.sum(moments, axis=1, keepdims=True)
    mu = [total[m : m + 1] for m in range(2 * ITERS + 1)]

    def inner_product(left, right):
        value = None
        for i, a in enumerate(left):
            for j, b in enumerate(right):
                if a is not None and b is not None:
                    term = a * b * mu[i + j]
                    value = term if value is None else value + term
        return value

    def plus(left, scale, right):
        if right is None:
            return left
        return scale * right if left is None else left + scale * right

    one = jnp.ones((1, 1), f32)
    resid = [one, None, None, None]
    direct = [one, None, None, None]
    field = [None, None, None, None]
    rz = mu[0]
    for it in range(ITERS):
        moved = [None] + direct[:-1]
        alpha = rz / inner_product(direct, moved)
        field = [plus(a, alpha, b) for a, b in zip(field, direct)]
        resid = [plus(a, -alpha, b) for a, b in zip(resid, moved)]
        if it + 1 < ITERS:
            new = inner_product(resid, resid)
            beta = new / rz
            direct = [plus(a, beta, b) for a, b in zip(resid, direct)]
            rz = new
    out_field = field[0] * basis_ref[0]
    for i in range(1, ITERS):
        out_field = out_field + field[i] * basis_ref[i]
    out_resid = image_ref[0]
    for i in range(1, ITERS + 1):
        out_resid = out_resid + resid[i] * image_ref[i]
    field_ref[...] = out_field
    resid_ref[...] = out_resid
    for copy in first + in_flight:
        copy.wait_send()


def local(delta_flux, noise_var, pixel_pos, pixel_count, pair_list):
    slots = pair_list.shape[3]
    n_sky = lax.axis_size("sky")
    n_gz = lax.axis_size("gz")
    n_outer = n_sky // INNER
    vmem = pl.BlockSpec(memory_space=pltpu.VMEM)
    hbm = pl.BlockSpec(memory_space=pltpu.HBM)
    shape = jax.ShapeDtypeStruct((BLOCKS, WIDTH), f32)
    dma = pltpu.SemaphoreType.DMA
    field, resid = pl.pallas_call(
        functools.partial(body, slots),
        out_shape=(shape, shape),
        in_specs=[hbm] * 5,
        out_specs=(vmem, vmem),
        scratch_shapes=[
            pltpu.VMEM((BLOCKS, WIDTH), f32),
            pltpu.VMEM((BLOCKS, WIDTH), f32),
            pltpu.VMEM((3, BLOCKS, WIDTH), f32),
            pltpu.VMEM((1, BLOCKS), jnp.int32),
            pltpu.VMEM((3, 1, slots), jnp.int32),
            pltpu.VMEM((SUB, slots), jnp.int32),
            pltpu.SMEM((SUB, slots), jnp.int32),
            pltpu.VMEM((BLOCKS, WIDTH, WIDTH), bf16),
            pltpu.VMEM((slots + BLOCKS, WIDTH, WIDTH), f32),
            pltpu.VMEM((slots, WIDTH, WIDTH), f32),
            pltpu.VMEM((BLOCKS, WIDTH, WIDTH), f32),
            pltpu.VMEM((CODES, 3, BLOCKS, WIDTH), f32),
            pltpu.VMEM((CODES, BLOCKS, WIDTH), f32),
            pltpu.VMEM((CODES, BLOCKS, WIDTH), f32),
            pltpu.VMEM((CODES, BLOCKS, WIDTH), f32),
            pltpu.VMEM((ITERS, CODES, 2 * BLOCKS, WIDTH), f32),
            pltpu.VMEM((ITERS, CODES, 2 * BLOCKS, WIDTH), f32),
            pltpu.VMEM((slots, WIDTH), f32),
            pltpu.VMEM((BLOCKS, WIDTH), f32),
            pltpu.VMEM((ITERS + 1, BLOCKS, WIDTH), f32),
            pltpu.VMEM((ITERS + 1, BLOCKS, WIDTH), f32),
            pltpu.VMEM((CODES * BLOCKS, 2 * slots), bf16),
            pltpu.VMEM((3, SUB, WIDTH), f32),
            pltpu.VMEM((n_gz - 1, SUB, WIDTH), f32),
            pltpu.VMEM((INNER - 1, SUB, WIDTH), f32),
            pltpu.VMEM((n_outer - 1, SUB, WIDTH), f32),
            dma((6,)), dma((CODES,)), dma((CODES,)),
            dma((ITERS, CODES)), dma((ITERS, CODES)),
            dma((ITERS, CODES)), dma((ITERS, CODES)),
            dma((n_gz - 1,)), dma((n_gz - 1,)),
            dma((INNER - 1,)), dma((INNER - 1,)),
            dma((n_outer - 1,)), dma((n_outer - 1,)),
        ],
        compiler_params=pltpu.CompilerParams(
            collective_id=0, has_side_effects=True, vmem_limit_bytes=40 * 1024 * 1024
        ),
    )(
        *(
            pltpu.with_memory_space_constraint(value, pltpu.HBM)
            for value in (
                delta_flux, noise_var, pixel_pos, pixel_count, jnp.transpose(pair_list, (0, 2, 1, 3))
            )
        )
    )
    return field[None, None], resid[None, None]


def solution(mesh):
    placed = (
        P("sky", "gz", None, None),
        P("sky", "gz", None, None),
        P("sky", "gz", None, None, None),
        P("sky", "gz", None),
        P("sky", "gz", None, None),
    )
    return jax.shard_map(
        local,
        mesh=mesh,
        in_specs=placed,
        out_specs=(P("sky", "gz", None, None), P("sky", "gz", None, None)),
        check_vma=False,
    )
```

```python
import functools
import math
import jax
import jax.numpy as jnp
from jax import lax
from jax.experimental import pallas as pl
from jax.experimental.pallas import tpu as pltpu
from jax.sharding import PartitionSpec as P

ITERS = 3
BLOCKS = 32
WIDTH = 128
CODES = 9
OWN = 4
SUB = 8
INNER = 8

signal_amp = 0.25
bf16 = jnp.bfloat16
f32 = jnp.float32


def mm(left, right):
    return lax.dot_general(left, right, (((1,), (0,)), ((), ())), preferred_element_type=f32)


def mm_trans(left, right):
    return lax.dot_general(left, right, (((1,), (1,)), ((), ())), preferred_element_type=f32)


def split_two(values):
    high = values.astype(bf16)
    return high, (values - high.astype(f32)).astype(bf16)


def split_three(values):
    high = values.astype(bf16).astype(f32)
    rest = values - high
    mid = rest.astype(bf16).astype(f32)
    return high, mid, rest - mid


def body(
    slots,
    delta_in, noise_in, pos_in, count_in, pair_in,
    field_ref, resid_ref,
    delta_ref, noise_ref, pos_ref, count_ref, pair_ref, order_ref, spair_ref,
    near_ref, cov_ref, running_ref, column_ref, first_ref, halo0_ref, halo1_ref, halo2_ref, owed_ref, got_ref,
    pay_ref, self_ref, basis_ref, image_ref, from_ref,
    sum_ref, red1_ref, red2_ref, red3_ref,
    load_sem, first_send, first_recv, halo_send, halo_recv, owed_send, owed_recv,
    red1_send, red1_recv, red2_send, red2_recv, red3_send, red3_recv,
):
    n_sky = lax.axis_size("sky")
    n_gz = lax.axis_size("gz")
    n_outer = n_sky // INNER
    me_s = lax.axis_index("sky")
    me_g = lax.axis_index("gz")
    outer = me_s // INNER
    inner = me_s % INNER

    def tile_at(code):
        return (
            (me_s + code // 3 - 1 + n_sky) % n_sky,
            (me_g + code % 3 - 1 + n_gz) % n_gz,
        )

    def gz_at(step):
        return (me_s, (me_g + step) % n_gz)

    def inner_at(step):
        return (outer * INNER + (inner + step) % INNER, me_g)

    def outer_at(step):
        return ((outer + step) % n_outer * INNER + inner, me_g)

    sides = (0, 2, 6, 8, 1, 7, 3, 5)
    partners = [tile_at(code) for code in sides]
    partners += [gz_at(step) for step in range(2, n_gz - 1)]
    partners += [inner_at(step) for step in range(1, INNER)]
    partners += [outer_at(step) for step in range(1, n_outer)]
    loads = [
        pltpu.make_async_copy(source, into, load_sem.at[i])
        for i, (source, into) in enumerate(
            (
                (pos_in.at[0, 0], pos_ref),
                (pair_in.at[0], pair_ref),
                (count_in.at[0], count_ref),
                (noise_in.at[0, 0], noise_ref),
                (delta_in.at[0, 0], delta_ref),
            )
        )
    ]
    for copy in loads:
        copy.start()
    barrier = pltpu.get_barrier_semaphore()
    for partner in partners:
        pl.semaphore_signal(
            barrier, inc=1, device_id=partner, device_id_type=pl.DeviceIdType.MESH
        )

    def remote(source, target, send, recv, device):
        return pltpu.make_async_remote_copy(
            src_ref=source, dst_ref=target, send_sem=send, recv_sem=recv,
            device_id=device, device_id_type=pl.DeviceIdType.MESH,
        )

    loads[0].wait()
    first_ref[OWN] = pos_ref[...]

    sub = lax.broadcasted_iota(jnp.int32, (SUB, WIDTH), 0)
    mid_x = (2 * me_s + 1).astype(f32)
    mid_z = (4 * me_g + 2).astype(f32)
    scale = math.sqrt(math.log2(math.e))
    def features(code, block, swap):
        x = (first_ref[code, 0, pl.ds(block, 1), :] - mid_x) * scale
        y = (first_ref[code, 1, pl.ds(block, 1), :] - 1.0) * scale
        z = (first_ref[code, 2, pl.ds(block, 1), :] - mid_z) * scale
        size = -0.5 * (x * x + y * y + z * z)
        tile = jnp.where(sub == 0, x, 0.0)
        tile = jnp.where(sub == 1, y, tile)
        tile = jnp.where(sub == 2, z, tile)
        tile = jnp.where(sub == (3 if swap else 4), size, tile)
        return jnp.where(sub == (4 if swap else 3), 1.0, tile)

    blank = jnp.zeros((WIDTH - 6 * SUB, WIDTH), f32)
    depth = 6 * SUB

    def near_step(step, _):
        for k in range(4):
            block = step * 4 + k
            h, m, l = split_three(features(OWN, block, True))
            stack = jnp.concatenate([h, h, m, m, h, l, blank], axis=0)
            near_ref[block] = jnp.transpose(stack).astype(bf16)
        return 0

    lax.fori_loop(0, BLOCKS // 4, near_step, 0)

    pl.semaphore_wait(barrier, len(partners))
    first = [
        remote(pos_ref, first_ref.at[8 - c], first_send.at[c], first_recv.at[8 - c], tile_at(c))
        for c in sides
    ]
    for copy in first:
        copy.start()
    for copy in loads[1:]:
        copy.wait()

    def halo_copies(it, into):
        return [
            remote(
                basis_ref.at[it], into.at[8 - c],
                halo_send.at[it, c], halo_recv.at[it, 8 - c], tile_at(c),
            )
            for c in sides
        ]

    eye_b = lax.broadcasted_iota(jnp.int32, (BLOCKS, BLOCKS), 0) == lax.broadcasted_iota(
        jnp.int32, (BLOCKS, BLOCKS), 1
    )
    count = jnp.sum(
        jnp.where(eye_b, count_ref[...].astype(f32), 0.0), axis=1, keepdims=True
    )
    lanes = lax.broadcasted_iota(jnp.int32, (BLOCKS, WIDTH), 1).astype(f32)
    live = (lanes < count).astype(f32)
    noise = noise_ref[...]
    precond = 1.0 / (noise + signal_amp)
    right_side = live * delta_ref[...]
    image_ref[0] = right_side
    basis_ref[0] = precond * right_side

    halo_refs = (halo0_ref, halo1_ref, halo2_ref)
    arriving = halo_copies(0, halo0_ref)
    for copy in arriving:
        copy.start()
    halo0_ref[OWN] = basis_ref[0]

    shape = (slots, slots)
    rows_s = lax.broadcasted_iota(jnp.int32, shape, 0)
    lanes_s = lax.broadcasted_iota(jnp.int32, shape, 1)
    codes = pair_ref[0]
    near_row = (codes >= 3).astype(jnp.int32) + (codes >= 6).astype(jnp.int32)
    row_s = me_s + near_row - 1
    row_g = me_g + (codes - 3 * near_row) - 1
    filled = codes < CODES
    inside = filled & (row_s >= 0) & (row_s < n_sky) & (row_g >= 0) & (row_g < n_gz)
    target = pair_ref[2]
    target_col = jnp.sum(jnp.where(rows_s == lanes_s, target, 0), axis=1, keepdims=True)
    before = (target < target_col) | ((target == target_col) & (lanes_s < rows_s))
    rank = jnp.sum(before.astype(jnp.int32), axis=1, keepdims=True)
    place = rank == lanes_s
    fields = (jnp.minimum(codes, CODES - 1), pair_ref[1], target, inside.astype(jnp.int32))
    limits = (CODES - 1, BLOCKS - 1, BLOCKS - 1, 1)
    table = jnp.zeros((SUB, slots), jnp.int32)
    for i, (field, limit) in enumerate(zip(fields, limits)):
        column = jnp.sum(jnp.where(rows_s == lanes_s, field, 0), axis=1, keepdims=True)
        moved = jnp.sum(jnp.where(place, column, 0), axis=0, keepdims=True)
        table = jnp.where(sub == i, jnp.clip(moved, 0, limit), table)
    ends = jnp.sum((target_col <= lanes_s).astype(jnp.int32), axis=0, keepdims=True)
    table = jnp.where(sub == len(fields), jnp.clip(ends, 0, slots), table)
    order_ref[...] = table
    to_scalar = pltpu.make_async_copy(order_ref, spair_ref, load_sem.at[5])
    to_scalar.start()

    flat = table[0:1] * BLOCKS + table[1:2]
    weight = table[3:4].astype(f32) * signal_amp
    hits = lax.broadcasted_iota(jnp.int32, (BLOCKS, slots), 0) == target
    named = jnp.sum(
        jnp.where(hits & filled, signal_amp, 0.0), axis=1, keepdims=True
    )
    rows_f = lax.broadcasted_iota(jnp.int32, (CODES * BLOCKS, slots), 0)
    backs = jnp.where(rows_f == flat, weight, 0.0)
    from_ref[:, :slots] = backs.astype(bf16)
    from_ref[:, slots:] = backs.astype(bf16)
    sourced = jnp.broadcast_to(
        jnp.sum(backs, axis=1, keepdims=True), (CODES * BLOCKS, WIDTH)
    )
    for c in range(CODES):
        owed_ref[0, c, BLOCKS:] = sourced[c * BLOCKS : (c + 1) * BLOCKS]

    def spread(values):
        for block in range(BLOCKS):
            column_ref[block] = jnp.transpose(
                jnp.broadcast_to(values[block : block + 1], (WIDTH, WIDTH))
            )

    spread(basis_ref[0])

    def make_tile(slot, block, code, source):
        h, m, l = split_three(features(code, source, False))
        stack = jnp.concatenate([h, m, h, m, l, h], axis=0).astype(bf16)
        cov_ref[slot] = jnp.exp2(mm(near_ref[block, :, :depth], stack))

    def self_tile(step, _):
        for k in range(4):
            block = step * 4 + k
            make_tile(slots + block, block, OWN, block)
        return 0

    lax.fori_loop(0, BLOCKS // 4, self_tile, 0)
    to_scalar.wait()
    for copy in first:
        copy.wait_recv()

    def down(slot, block):
        product = cov_ref[slot] * column_ref[block]
        return jnp.sum(
            jnp.sum(product.reshape(WIDTH // SUB, SUB, WIDTH), axis=0), axis=0, keepdims=True
        )

    def doubled(values):
        high, low = split_two(values)
        return jnp.concatenate([high, low], axis=0)

    lanes_sq = lax.broadcasted_iota(jnp.int32, (WIDTH, WIDTH), 1)
    in_flight = []
    own_weight = None
    for it in range(ITERS):
        vector = basis_ref[it]
        halo_ref = halo_refs[it]
        if it > 0:
            arriving = halo_copies(it, halo_ref)
            for copy in arriving:
                copy.start()
            halo_ref[OWN] = vector

        if it > 0:
            spread(vector)

        if it == 0:

            def pair_tile(step, _):
                for k in range(32):
                    slot = step * 32 + k
                    make_tile(slot, spair_ref[2, slot], spair_ref[0, slot], spair_ref[1, slot])
                return 0

            lax.fori_loop(0, slots // 32, pair_tile, 0)

        def pay_step(step, _):
            total = jnp.zeros((SUB, WIDTH), f32)
            for k in range(SUB):
                slot = step * SUB + k
                total = jnp.where(sub == k, down(slot, spair_ref[2, slot]), total)
            pay_ref[pl.ds(step * SUB, SUB), :] = total
            return 0

        lax.fori_loop(0, slots // SUB, pay_step, 0)
        owed = mm(from_ref[...], doubled(pay_ref[...]))
        for c in range(CODES):
            owed_ref[it, c, 0:BLOCKS] = owed[c * BLOCKS : (c + 1) * BLOCKS]
        extent = 2 * BLOCKS if it == 0 else BLOCKS
        returns = [
            remote(
                owed_ref.at[it, c, pl.ds(0, extent)], got_ref.at[it, 8 - c, pl.ds(0, extent)],
                owed_send.at[it, c], owed_recv.at[it, 8 - c], tile_at(c),
            )
            for c in sides
        ]
        for copy in returns:
            copy.start()

        def self_step(step, _):
            total = jnp.zeros((SUB, WIDTH), f32)
            for k in range(SUB):
                block = step * SUB + k
                total = jnp.where(sub == k, down(slots + block, block), total)
            self_ref[pl.ds(step * SUB, SUB), :] = total
            return 0

        lax.fori_loop(0, BLOCKS // SUB, self_step, 0)
        for copy in arriving:
            copy.wait_recv()

        def gain_step(step, running):
            for k in range(SUB):
                slot = step * SUB + k
                row = halo_ref[spair_ref[0, slot], pl.ds(spair_ref[1, slot], 1), :]
                row = row * (spair_ref[3, slot].astype(f32) * signal_amp)
                same = spair_ref[2, slot] == spair_ref[2, jnp.maximum(slot - 1, 0)]
                running = running * same.astype(f32) + cov_ref[slot] * row
                running_ref[slot] = running
            return running

        lax.fori_loop(0, slots // SUB, gain_step, jnp.zeros((WIDTH, WIDTH), f32))
        tall = jnp.zeros((WIDTH, WIDTH), f32)
        for block in range(BLOCKS):
            end = spair_ref[4, block]
            start = spair_ref[4, block - 1] if block > 0 else 0
            reach = jnp.sum(running_ref[jnp.clip(end - 1, 0, slots - 1)], axis=1, keepdims=True)
            reach = reach * (end > start).astype(f32)
            tall = jnp.where(lanes_sq == block, reach, tall)
        totals = jnp.transpose(tall)[:BLOCKS]
        totals = totals + owed_ref[it, OWN, 0:BLOCKS]
        for copy in returns:
            copy.wait_recv()
        for c in sides:
            totals = totals + got_ref[it, c, 0:BLOCKS]
        if it == 0:
            own_weight = owed_ref[0, OWN, BLOCKS:] + (signal_amp + named)
            for c in sides:
                own_weight = own_weight + got_ref[0, c, BLOCKS:]
        totals = totals + own_weight * self_ref[...]
        image = live * totals + noise * vector
        image_ref[it + 1] = image
        basis_ref[it + 1] = precond * image
        in_flight += arriving + returns

    moments = jnp.zeros((SUB, WIDTH), f32)
    for m in range(2 * ITERS + 1):
        product = basis_ref[m // 2] * image_ref[m - m // 2]
        moments = jnp.where(sub == m, jnp.sum(product, axis=0, keepdims=True), moments)
    stages = (
        (gz_at, n_gz, red1_ref, red1_send, red1_recv),
        (inner_at, INNER, red2_ref, red2_send, red2_recv),
        (outer_at, n_outer, red3_ref, red3_send, red3_recv),
    )
    for stage, (device_at, members, into, send, recv) in enumerate(stages):
        sum_ref[stage] = moments
        copies = [
            remote(
                sum_ref.at[stage], into.at[step - 1], send.at[step - 1], recv.at[step - 1],
                device_at(step),
            )
            for step in range(1, members)
        ]
        for copy in copies:
            copy.start()
        for step, copy in enumerate(copies):
            copy.wait_recv()
            moments = moments + into[step]
        in_flight += copies
    total = jnp.sum(moments, axis=1, keepdims=True)
    mu = [total[m : m + 1] for m in range(2 * ITERS + 1)]

    def inner_product(left, right):
        value = None
        for i, a in enumerate(left):
            for j, b in enumerate(right):
                if a is not None and b is not None:
                    term = a * b * mu[i + j]
                    value = term if value is None else value + term
        return value

    def plus(left, scale, right):
        if right is None:
            return left
        return scale * right if left is None else left + scale * right

    one = jnp.ones((1, 1), f32)
    resid = [one, None, None, None]
    direct = [one, None, None, None]
    field = [None, None, None, None]
    rz = mu[0]
    for it in range(ITERS):
        moved = [None] + direct[:-1]
        alpha = rz / inner_product(direct, moved)
        field = [plus(a, alpha, b) for a, b in zip(field, direct)]
        resid = [plus(a, -alpha, b) for a, b in zip(resid, moved)]
        if it + 1 < ITERS:
            new = inner_product(resid, resid)
            beta = new / rz
            direct = [plus(a, beta, b) for a, b in zip(resid, direct)]
            rz = new
    out_field = field[0] * basis_ref[0]
    for i in range(1, ITERS):
        out_field = out_field + field[i] * basis_ref[i]
    out_resid = image_ref[0]
    for i in range(1, ITERS + 1):
        out_resid = out_resid + resid[i] * image_ref[i]
    field_ref[...] = out_field
    resid_ref[...] = out_resid
    for copy in first + in_flight:
        copy.wait_send()


def local(delta_flux, noise_var, pixel_pos, pixel_count, pair_list):
    slots = pair_list.shape[3]
    n_sky = lax.axis_size("sky")
    n_gz = lax.axis_size("gz")
    n_outer = n_sky // INNER
    vmem = pl.BlockSpec(memory_space=pltpu.VMEM)
    hbm = pl.BlockSpec(memory_space=pltpu.HBM)
    shape = jax.ShapeDtypeStruct((BLOCKS, WIDTH), f32)
    dma = pltpu.SemaphoreType.DMA
    field, resid = pl.pallas_call(
        functools.partial(body, slots),
        out_shape=(shape, shape),
        in_specs=[hbm] * 5,
        out_specs=(vmem, vmem),
        scratch_shapes=[
            pltpu.VMEM((BLOCKS, WIDTH), f32),
            pltpu.VMEM((BLOCKS, WIDTH), f32),
            pltpu.VMEM((3, BLOCKS, WIDTH), f32),
            pltpu.VMEM((1, BLOCKS), jnp.int32),
            pltpu.VMEM((3, 1, slots), jnp.int32),
            pltpu.VMEM((SUB, slots), jnp.int32),
            pltpu.SMEM((SUB, slots), jnp.int32),
            pltpu.VMEM((BLOCKS, WIDTH, WIDTH), bf16),
            pltpu.VMEM((slots + BLOCKS, WIDTH, WIDTH), f32),
            pltpu.VMEM((slots, WIDTH, WIDTH), f32),
            pltpu.VMEM((BLOCKS, WIDTH, WIDTH), f32),
            pltpu.VMEM((CODES, 3, BLOCKS, WIDTH), f32),
            pltpu.VMEM((CODES, BLOCKS, WIDTH), f32),
            pltpu.VMEM((CODES, BLOCKS, WIDTH), f32),
            pltpu.VMEM((CODES, BLOCKS, WIDTH), f32),
            pltpu.VMEM((ITERS, CODES, 2 * BLOCKS, WIDTH), f32),
            pltpu.VMEM((ITERS, CODES, 2 * BLOCKS, WIDTH), f32),
            pltpu.VMEM((slots, WIDTH), f32),
            pltpu.VMEM((BLOCKS, WIDTH), f32),
            pltpu.VMEM((ITERS + 1, BLOCKS, WIDTH), f32),
            pltpu.VMEM((ITERS + 1, BLOCKS, WIDTH), f32),
            pltpu.VMEM((CODES * BLOCKS, 2 * slots), bf16),
            pltpu.VMEM((3, SUB, WIDTH), f32),
            pltpu.VMEM((n_gz - 1, SUB, WIDTH), f32),
            pltpu.VMEM((INNER - 1, SUB, WIDTH), f32),
            pltpu.VMEM((n_outer - 1, SUB, WIDTH), f32),
            dma((6,)), dma((CODES,)), dma((CODES,)),
            dma((ITERS, CODES)), dma((ITERS, CODES)),
            dma((ITERS, CODES)), dma((ITERS, CODES)),
            dma((n_gz - 1,)), dma((n_gz - 1,)),
            dma((INNER - 1,)), dma((INNER - 1,)),
            dma((n_outer - 1,)), dma((n_outer - 1,)),
        ],
        compiler_params=pltpu.CompilerParams(
            collective_id=0, has_side_effects=True, vmem_limit_bytes=40 * 1024 * 1024
        ),
    )(
        *(
            pltpu.with_memory_space_constraint(value, pltpu.HBM)
            for value in (
                delta_flux, noise_var, pixel_pos, pixel_count, jnp.transpose(pair_list, (0, 2, 1, 3))
            )
        )
    )
    return field[None, None], resid[None, None]


def solution(mesh):
    placed = (
        P("sky", "gz", None, None),
        P("sky", "gz", None, None),
        P("sky", "gz", None, None, None),
        P("sky", "gz", None),
        P("sky", "gz", None, None),
    )
    return jax.shard_map(
        local,
        mesh=mesh,
        in_specs=placed,
        out_specs=(P("sky", "gz", None, None), P("sky", "gz", None, None)),
        check_vma=False,
    )
```

```python
import functools
import math
import jax
import jax.numpy as jnp
from jax import lax
from jax.experimental import pallas as pl
from jax.experimental.pallas import tpu as pltpu
from jax.sharding import PartitionSpec as P

ITERS = 3
BLOCKS = 32
WIDTH = 128
CODES = 9
OWN = 4
SUB = 8
INNER = 8

signal_amp = 0.25
bf16 = jnp.bfloat16
f32 = jnp.float32


def mm(left, right):
    return lax.dot_general(left, right, (((1,), (0,)), ((), ())), preferred_element_type=f32)


def mm_trans(left, right):
    return lax.dot_general(left, right, (((1,), (1,)), ((), ())), preferred_element_type=f32)


def split_two(values):
    high = values.astype(bf16)
    return high, (values - high.astype(f32)).astype(bf16)


def split_three(values):
    high = values.astype(bf16).astype(f32)
    rest = values - high
    mid = rest.astype(bf16).astype(f32)
    return high, mid, rest - mid


def body(
    slots,
    delta_in, noise_in, pos_in, count_in, pair_in,
    out_ref,
    delta_ref, noise_ref, pos_ref, count_ref, pair_ref, order_ref, spair_ref,
    near_ref, cov_ref, running_ref, column_ref, first_ref, halo0_ref, halo1_ref, halo2_ref, owed_ref, got_ref,
    pay_ref, self_ref, basis_ref, image_ref, from_ref,
    sum_ref, red1_ref, red2_ref, red3_ref,
    load_sem, first_send, first_recv, halo_send, halo_recv, owed_send, owed_recv,
    red1_send, red1_recv, red2_send, red2_recv, red3_send, red3_recv,
):
    n_sky = lax.axis_size("sky")
    n_gz = lax.axis_size("gz")
    n_outer = n_sky // INNER
    me_s = lax.axis_index("sky")
    me_g = lax.axis_index("gz")
    outer = me_s // INNER
    inner = me_s % INNER

    def tile_at(code):
        return (
            (me_s + code // 3 - 1 + n_sky) % n_sky,
            (me_g + code % 3 - 1 + n_gz) % n_gz,
        )

    def gz_at(step):
        return (me_s, (me_g + step) % n_gz)

    def inner_at(step):
        return (outer * INNER + (inner + step) % INNER, me_g)

    def outer_at(step):
        return ((outer + step) % n_outer * INNER + inner, me_g)

    sides = (0, 2, 6, 8, 1, 7, 3, 5)
    partners = [tile_at(code) for code in sides]
    partners += [gz_at(step) for step in range(2, n_gz - 1)]
    partners += [inner_at(step) for step in range(1, INNER)]
    partners += [outer_at(step) for step in range(1, n_outer)]
    loads = [
        pltpu.make_async_copy(source, into, load_sem.at[i])
        for i, (source, into) in enumerate(
            (
                (pos_in.at[0, 0], pos_ref),
                (pair_in.at[0], pair_ref),
                (count_in.at[0], count_ref),
                (noise_in.at[0, 0], noise_ref),
                (delta_in.at[0, 0], delta_ref),
            )
        )
    ]
    for copy in loads:
        copy.start()
    barrier = pltpu.get_barrier_semaphore()
    for partner in partners:
        pl.semaphore_signal(
            barrier, inc=1, device_id=partner, device_id_type=pl.DeviceIdType.MESH
        )

    def remote(source, target, send, recv, device):
        return pltpu.make_async_remote_copy(
            src_ref=source, dst_ref=target, send_sem=send, recv_sem=recv,
            device_id=device, device_id_type=pl.DeviceIdType.MESH,
        )

    loads[0].wait()
    first_ref[OWN] = pos_ref[...]

    sub = lax.broadcasted_iota(jnp.int32, (SUB, WIDTH), 0)
    mid_x = (2 * me_s + 1).astype(f32)
    mid_z = (4 * me_g + 2).astype(f32)
    scale = math.sqrt(math.log2(math.e))
    def features(code, block, swap):
        x = (first_ref[code, 0, pl.ds(block, 1), :] - mid_x) * scale
        y = (first_ref[code, 1, pl.ds(block, 1), :] - 1.0) * scale
        z = (first_ref[code, 2, pl.ds(block, 1), :] - mid_z) * scale
        size = -0.5 * (x * x + y * y + z * z)
        tile = jnp.where(sub == 0, x, 0.0)
        tile = jnp.where(sub == 1, y, tile)
        tile = jnp.where(sub == 2, z, tile)
        tile = jnp.where(sub == (3 if swap else 4), size, tile)
        return jnp.where(sub == (4 if swap else 3), 1.0, tile)

    blank = jnp.zeros((WIDTH - 6 * SUB, WIDTH), f32)
    depth = 6 * SUB

    def near_step(step, _):
        for k in range(4):
            block = step * 4 + k
            h, m, l = split_three(features(OWN, block, True))
            stack = jnp.concatenate([h, h, m, m, h, l, blank], axis=0)
            near_ref[block] = jnp.transpose(stack).astype(bf16)
        return 0

    lax.fori_loop(0, BLOCKS // 4, near_step, 0)

    pl.semaphore_wait(barrier, len(partners))
    first = [
        remote(pos_ref, first_ref.at[8 - c], first_send.at[c], first_recv.at[8 - c], tile_at(c))
        for c in sides
    ]
    for copy in first:
        copy.start()
    for copy in loads[1:]:
        copy.wait()

    def halo_copies(it, into):
        return [
            remote(
                basis_ref.at[it], into.at[8 - c],
                halo_send.at[it, c], halo_recv.at[it, 8 - c], tile_at(c),
            )
            for c in sides
        ]

    eye_b = lax.broadcasted_iota(jnp.int32, (BLOCKS, BLOCKS), 0) == lax.broadcasted_iota(
        jnp.int32, (BLOCKS, BLOCKS), 1
    )
    count = jnp.sum(
        jnp.where(eye_b, count_ref[...].astype(f32), 0.0), axis=1, keepdims=True
    )
    lanes = lax.broadcasted_iota(jnp.int32, (BLOCKS, WIDTH), 1).astype(f32)
    live = (lanes < count).astype(f32)
    noise = noise_ref[...]
    precond = 1.0 / (noise + signal_amp)
    right_side = live * delta_ref[...]
    image_ref[0] = right_side
    basis_ref[0] = precond * right_side

    halo_refs = (halo0_ref, halo1_ref, halo2_ref)
    arriving = halo_copies(0, halo0_ref)
    for copy in arriving:
        copy.start()
    halo0_ref[OWN] = basis_ref[0]

    shape = (slots, slots)
    rows_s = lax.broadcasted_iota(jnp.int32, shape, 0)
    lanes_s = lax.broadcasted_iota(jnp.int32, shape, 1)
    codes = pair_ref[0]
    near_row = (codes >= 3).astype(jnp.int32) + (codes >= 6).astype(jnp.int32)
    row_s = me_s + near_row - 1
    row_g = me_g + (codes - 3 * near_row) - 1
    filled = codes < CODES
    inside = filled & (row_s >= 0) & (row_s < n_sky) & (row_g >= 0) & (row_g < n_gz)
    target = pair_ref[2]
    target_col = jnp.sum(jnp.where(rows_s == lanes_s, target, 0), axis=1, keepdims=True)
    before = (target < target_col) | ((target == target_col) & (lanes_s < rows_s))
    rank = jnp.sum(before.astype(jnp.int32), axis=1, keepdims=True)
    place = rank == lanes_s
    fields = (jnp.minimum(codes, CODES - 1), pair_ref[1], target, inside.astype(jnp.int32))
    limits = (CODES - 1, BLOCKS - 1, BLOCKS - 1, 1)
    table = jnp.zeros((SUB, slots), jnp.int32)
    for i, (field, limit) in enumerate(zip(fields, limits)):
        column = jnp.sum(jnp.where(rows_s == lanes_s, field, 0), axis=1, keepdims=True)
        moved = jnp.sum(jnp.where(place, column, 0), axis=0, keepdims=True)
        table = jnp.where(sub == i, jnp.clip(moved, 0, limit), table)
    ends = jnp.sum((target_col <= lanes_s).astype(jnp.int32), axis=0, keepdims=True)
    table = jnp.where(sub == len(fields), jnp.clip(ends, 0, slots), table)
    order_ref[...] = table
    to_scalar = pltpu.make_async_copy(order_ref, spair_ref, load_sem.at[5])
    to_scalar.start()

    flat = table[0:1] * BLOCKS + table[1:2]
    weight = table[3:4].astype(f32) * signal_amp
    hits = lax.broadcasted_iota(jnp.int32, (BLOCKS, slots), 0) == target
    named = jnp.sum(
        jnp.where(hits & filled, signal_amp, 0.0), axis=1, keepdims=True
    )
    rows_f = lax.broadcasted_iota(jnp.int32, (CODES * BLOCKS, slots), 0)
    backs = jnp.where(rows_f == flat, weight, 0.0)
    from_ref[:, :slots] = backs.astype(bf16)
    from_ref[:, slots:] = backs.astype(bf16)
    sourced = jnp.broadcast_to(
        jnp.sum(backs, axis=1, keepdims=True), (CODES * BLOCKS, WIDTH)
    )
    for c in range(CODES):
        owed_ref[0, c, BLOCKS:] = sourced[c * BLOCKS : (c + 1) * BLOCKS]

    def spread(values):
        for block in range(BLOCKS):
            column_ref[block] = jnp.transpose(
                jnp.broadcast_to(values[block : block + 1], (WIDTH, WIDTH))
            )

    spread(basis_ref[0])

    def make_tile(slot, block, code, source):
        h, m, l = split_three(features(code, source, False))
        stack = jnp.concatenate([h, m, h, m, l, h], axis=0).astype(bf16)
        cov_ref[slot] = jnp.exp2(mm(near_ref[block, :, :depth], stack))

    def self_tile(step, _):
        for k in range(4):
            block = step * 4 + k
            make_tile(slots + block, block, OWN, block)
        return 0

    lax.fori_loop(0, BLOCKS // 4, self_tile, 0)
    to_scalar.wait()
    for copy in first:
        copy.wait_recv()

    def down(slot, block):
        product = cov_ref[slot] * column_ref[block]
        return jnp.sum(
            jnp.sum(product.reshape(WIDTH // SUB, SUB, WIDTH), axis=0), axis=0, keepdims=True
        )

    def doubled(values):
        high, low = split_two(values)
        return jnp.concatenate([high, low], axis=0)

    lanes_sq = lax.broadcasted_iota(jnp.int32, (WIDTH, WIDTH), 1)
    ones = jnp.ones((2 * WIDTH, WIDTH), bf16)
    in_flight = first
    own_weight = None
    for it in range(ITERS):
        vector = basis_ref[it]
        halo_ref = halo_refs[it]
        if it > 0:
            arriving = halo_copies(it, halo_ref)
            for copy in arriving:
                copy.start()
            halo_ref[OWN] = vector

        if it > 0:
            spread(vector)

        if it == 0:

            def pair_tile(step, _):
                for k in range(32):
                    slot = step * 32 + k
                    make_tile(slot, spair_ref[2, slot], spair_ref[0, slot], spair_ref[1, slot])
                return 0

            lax.fori_loop(0, slots // 32, pair_tile, 0)

        def pay_step(step, _):
            total = jnp.zeros((SUB, WIDTH), f32)
            for k in range(SUB):
                slot = step * SUB + k
                total = jnp.where(sub == k, down(slot, spair_ref[2, slot]), total)
            pay_ref[pl.ds(step * SUB, SUB), :] = total
            return 0

        lax.fori_loop(0, slots // SUB, pay_step, 0)
        owed = mm(from_ref[...], doubled(pay_ref[...]))
        for c in range(CODES):
            owed_ref[it, c, 0:BLOCKS] = owed[c * BLOCKS : (c + 1) * BLOCKS]
        extent = 2 * BLOCKS if it == 0 else BLOCKS
        returns = [
            remote(
                owed_ref.at[it, c, pl.ds(0, extent)], got_ref.at[it, 8 - c, pl.ds(0, extent)],
                owed_send.at[it, c], owed_recv.at[it, 8 - c], tile_at(c),
            )
            for c in sides
        ]
        for copy in returns:
            copy.start()

        def self_step(step, _):
            total = jnp.zeros((SUB, WIDTH), f32)
            for k in range(SUB):
                block = step * SUB + k
                total = jnp.where(sub == k, down(slots + block, block), total)
            self_ref[pl.ds(step * SUB, SUB), :] = total
            return 0

        lax.fori_loop(0, BLOCKS // SUB, self_step, 0)
        for copy in arriving:
            copy.wait_recv()

        def gain_step(step, running):
            for k in range(SUB):
                slot = step * SUB + k
                row = halo_ref[spair_ref[0, slot], pl.ds(spair_ref[1, slot], 1), :]
                row = row * (spair_ref[3, slot].astype(f32) * signal_amp)
                same = spair_ref[2, slot] == spair_ref[2, jnp.maximum(slot - 1, 0)]
                running = running * same.astype(f32) + cov_ref[slot] * row
                running_ref[slot] = running
            return running

        lax.fori_loop(0, slots // SUB, gain_step, jnp.zeros((WIDTH, WIDTH), f32))
        tall = jnp.zeros((WIDTH, WIDTH), f32)
        for block in range(BLOCKS):
            end = spair_ref[4, block]
            start = spair_ref[4, block - 1] if block > 0 else 0
            sums = running_ref[jnp.clip(end - 1, 0, slots - 1)]
            if block % 3 == 0:
                high, low = split_two(sums)
                reach = mm(jnp.concatenate([high, low], axis=1), ones)
            else:
                reach = jnp.sum(sums, axis=1, keepdims=True)
            reach = reach * (end > start).astype(f32)
            tall = jnp.where(lanes_sq == block, reach, tall)
        totals = jnp.transpose(tall)[:BLOCKS]
        totals = totals + owed_ref[it, OWN, 0:BLOCKS]
        for copy in returns:
            copy.wait_recv()
        for c in sides:
            totals = totals + got_ref[it, c, 0:BLOCKS]
        if it == 0:
            own_weight = owed_ref[0, OWN, BLOCKS:] + (signal_amp + named)
            for c in sides:
                own_weight = own_weight + got_ref[0, c, BLOCKS:]
        totals = totals + own_weight * self_ref[...]
        image = live * totals + noise * vector
        image_ref[it + 1] = image
        basis_ref[it + 1] = precond * image
        in_flight = in_flight + arriving + returns

    moments = jnp.zeros((SUB, WIDTH), f32)
    for m in range(2 * ITERS + 1):
        product = basis_ref[m // 2] * image_ref[m - m // 2]
        moments = jnp.where(sub == m, jnp.sum(product, axis=0, keepdims=True), moments)
    stages = (
        (gz_at, n_gz, red1_ref, red1_send, red1_recv),
        (inner_at, INNER, red2_ref, red2_send, red2_recv),
        (outer_at, n_outer, red3_ref, red3_send, red3_recv),
    )
    for stage, (device_at, members, into, send, recv) in enumerate(stages):
        sum_ref[stage] = moments
        copies = [
            remote(
                sum_ref.at[stage], into.at[step - 1], send.at[step - 1], recv.at[step - 1],
                device_at(step),
            )
            for step in range(1, members)
        ]
        for copy in copies:
            copy.start()
        for copy in in_flight:
            copy.wait_send()
        in_flight = copies
        for step, copy in enumerate(copies):
            copy.wait_recv()
            moments = moments + into[step]
    total = jnp.sum(moments, axis=1, keepdims=True)
    mu = [total[m : m + 1] for m in range(2 * ITERS + 1)]

    def inner_product(left, right):
        value = None
        for i, a in enumerate(left):
            for j, b in enumerate(right):
                if a is not None and b is not None:
                    term = a * b * mu[i + j]
                    value = term if value is None else value + term
        return value

    def plus(left, scale, right):
        if right is None:
            return left
        return scale * right if left is None else left + scale * right

    one = jnp.ones((1, 1), f32)
    resid = [one, None, None, None]
    direct = [one, None, None, None]
    field = [None, None, None, None]
    rz = mu[0]
    for it in range(ITERS):
        moved = [None] + direct[:-1]
        alpha = rz / inner_product(direct, moved)
        field = [plus(a, alpha, b) for a, b in zip(field, direct)]
        resid = [plus(a, -alpha, b) for a, b in zip(resid, moved)]
        if it + 1 < ITERS:
            new = inner_product(resid, resid)
            beta = new / rz
            direct = [plus(a, beta, b) for a, b in zip(resid, direct)]
            rz = new
    out_field = field[0] * basis_ref[0]
    for i in range(1, ITERS):
        out_field = out_field + field[i] * basis_ref[i]
    out_resid = image_ref[0]
    for i in range(1, ITERS + 1):
        out_resid = out_resid + resid[i] * image_ref[i]
    out_ref[0] = out_field
    out_ref[1] = out_resid
    for copy in in_flight:
        copy.wait_send()


def local(delta_flux, noise_var, pixel_pos, pixel_count, pair_list):
    slots = pair_list.shape[3]
    n_sky = lax.axis_size("sky")
    n_gz = lax.axis_size("gz")
    n_outer = n_sky // INNER
    vmem = pl.BlockSpec(memory_space=pltpu.VMEM)
    hbm = pl.BlockSpec(memory_space=pltpu.HBM)
    shape = jax.ShapeDtypeStruct((2, BLOCKS, WIDTH), f32)
    dma = pltpu.SemaphoreType.DMA
    both = pl.pallas_call(
        functools.partial(body, slots),
        out_shape=shape,
        in_specs=[hbm] * 5,
        out_specs=vmem,
        scratch_shapes=[
            pltpu.VMEM((BLOCKS, WIDTH), f32),
            pltpu.VMEM((BLOCKS, WIDTH), f32),
            pltpu.VMEM((3, BLOCKS, WIDTH), f32),
            pltpu.VMEM((1, BLOCKS), jnp.int32),
            pltpu.VMEM((3, 1, slots), jnp.int32),
            pltpu.VMEM((SUB, slots), jnp.int32),
            pltpu.SMEM((SUB, slots), jnp.int32),
            pltpu.VMEM((BLOCKS, WIDTH, WIDTH), bf16),
            pltpu.VMEM((slots + BLOCKS, WIDTH, WIDTH), f32),
            pltpu.VMEM((slots, WIDTH, WIDTH), f32),
            pltpu.VMEM((BLOCKS, WIDTH, WIDTH), f32),
            pltpu.VMEM((CODES, 3, BLOCKS, WIDTH), f32),
            pltpu.VMEM((CODES, BLOCKS, WIDTH), f32),
            pltpu.VMEM((CODES, BLOCKS, WIDTH), f32),
            pltpu.VMEM((CODES, BLOCKS, WIDTH), f32),
            pltpu.VMEM((ITERS, CODES, 2 * BLOCKS, WIDTH), f32),
            pltpu.VMEM((ITERS, CODES, 2 * BLOCKS, WIDTH), f32),
            pltpu.VMEM((slots, WIDTH), f32),
            pltpu.VMEM((BLOCKS, WIDTH), f32),
            pltpu.VMEM((ITERS + 1, BLOCKS, WIDTH), f32),
            pltpu.VMEM((ITERS + 1, BLOCKS, WIDTH), f32),
            pltpu.VMEM((CODES * BLOCKS, 2 * slots), bf16),
            pltpu.VMEM((3, SUB, WIDTH), f32),
            pltpu.VMEM((n_gz - 1, SUB, WIDTH), f32),
            pltpu.VMEM((INNER - 1, SUB, WIDTH), f32),
            pltpu.VMEM((n_outer - 1, SUB, WIDTH), f32),
            dma((6,)), dma((CODES,)), dma((CODES,)),
            dma((ITERS, CODES)), dma((ITERS, CODES)),
            dma((ITERS, CODES)), dma((ITERS, CODES)),
            dma((n_gz - 1,)), dma((n_gz - 1,)),
            dma((INNER - 1,)), dma((INNER - 1,)),
            dma((n_outer - 1,)), dma((n_outer - 1,)),
        ],
        compiler_params=pltpu.CompilerParams(
            collective_id=0, has_side_effects=True, vmem_limit_bytes=40 * 1024 * 1024
        ),
    )(
        *(
            pltpu.with_memory_space_constraint(value, pltpu.HBM)
            for value in (
                delta_flux, noise_var, pixel_pos, pixel_count, jnp.transpose(pair_list, (0, 2, 1, 3))
            )
        )
    )
    return both[0][None, None], both[1][None, None]


def solution(mesh):
    placed = (
        P("sky", "gz", None, None),
        P("sky", "gz", None, None),
        P("sky", "gz", None, None, None),
        P("sky", "gz", None),
        P("sky", "gz", None, None),
    )
    return jax.shard_map(
        local,
        mesh=mesh,
        in_specs=placed,
        out_specs=(P("sky", "gz", None, None), P("sky", "gz", None, None)),
        check_vma=False,
    )
```

```python
import functools
import math
import jax
import jax.numpy as jnp
from jax import lax
from jax.experimental import pallas as pl
from jax.experimental.pallas import tpu as pltpu
from jax.sharding import PartitionSpec as P

ITERS = 3
BLOCKS = 32
WIDTH = 128
CODES = 9
OWN = 4
SUB = 8
INNER = 8

signal_amp = 0.25
bf16 = jnp.bfloat16
f32 = jnp.float32


def mm(left, right):
    return lax.dot_general(left, right, (((1,), (0,)), ((), ())), preferred_element_type=f32)


def mm_trans(left, right):
    return lax.dot_general(left, right, (((1,), (1,)), ((), ())), preferred_element_type=f32)


def split_two(values):
    high = values.astype(bf16)
    return high, (values - high.astype(f32)).astype(bf16)


def split_three(values):
    high = values.astype(bf16).astype(f32)
    rest = values - high
    mid = rest.astype(bf16).astype(f32)
    return high, mid, rest - mid


def body(
    slots,
    delta_in, noise_in, pos_in, count_in, pair_in,
    out_ref,
    delta_ref, noise_ref, pos_ref, count_ref, pair_ref, order_ref, spair_ref,
    near_ref, cov_ref, running_ref, column_ref, first_ref, halo0_ref, halo1_ref, halo2_ref, owed_ref, got_ref,
    pay_ref, self_ref, basis_ref, image_ref, from_ref,
    sum_ref, red1_ref, red2_ref, red3_ref,
    load_sem, first_send, first_recv, halo_send, halo_recv, owed_send, owed_recv,
    red1_send, red1_recv, red2_send, red2_recv, red3_send, red3_recv,
):
    n_sky = lax.axis_size("sky")
    n_gz = lax.axis_size("gz")
    n_outer = n_sky // INNER
    me_s = lax.axis_index("sky")
    me_g = lax.axis_index("gz")
    outer = me_s // INNER
    inner = me_s % INNER

    def tile_at(code):
        return (
            (me_s + code // 3 - 1 + n_sky) % n_sky,
            (me_g + code % 3 - 1 + n_gz) % n_gz,
        )

    def gz_at(step):
        return (me_s, (me_g + step) % n_gz)

    def inner_at(step):
        return (outer * INNER + (inner + step) % INNER, me_g)

    def outer_at(step):
        return ((outer + step) % n_outer * INNER + inner, me_g)

    sides = (0, 2, 6, 8, 1, 7, 3, 5)
    partners = [tile_at(code) for code in sides]
    partners += [gz_at(step) for step in range(2, n_gz - 1)]
    partners += [inner_at(step) for step in range(1, INNER)]
    partners += [outer_at(step) for step in range(1, n_outer)]
    loads = [
        pltpu.make_async_copy(source, into, load_sem.at[i])
        for i, (source, into) in enumerate(
            (
                (pos_in.at[0, 0], pos_ref),
                (pair_in.at[0], pair_ref),
                (count_in.at[0], count_ref),
                (noise_in.at[0, 0], noise_ref),
                (delta_in.at[0, 0], delta_ref),
            )
        )
    ]
    for copy in loads:
        copy.start()
    barrier = pltpu.get_barrier_semaphore()
    for partner in partners:
        pl.semaphore_signal(
            barrier, inc=1, device_id=partner, device_id_type=pl.DeviceIdType.MESH
        )

    def remote(source, target, send, recv, device):
        return pltpu.make_async_remote_copy(
            src_ref=source, dst_ref=target, send_sem=send, recv_sem=recv,
            device_id=device, device_id_type=pl.DeviceIdType.MESH,
        )

    loads[0].wait()
    first_ref[OWN] = pos_ref[...]

    sub = lax.broadcasted_iota(jnp.int32, (SUB, WIDTH), 0)
    mid_x = (2 * me_s + 1).astype(f32)
    mid_z = (4 * me_g + 2).astype(f32)
    scale = math.sqrt(math.log2(math.e))
    def features(code, block, swap):
        x = (first_ref[code, 0, pl.ds(block, 1), :] - mid_x) * scale
        y = (first_ref[code, 1, pl.ds(block, 1), :] - 1.0) * scale
        z = (first_ref[code, 2, pl.ds(block, 1), :] - mid_z) * scale
        size = -0.5 * (x * x + y * y + z * z)
        tile = jnp.where(sub == 0, x, 0.0)
        tile = jnp.where(sub == 1, y, tile)
        tile = jnp.where(sub == 2, z, tile)
        tile = jnp.where(sub == (3 if swap else 4), size, tile)
        return jnp.where(sub == (4 if swap else 3), 1.0, tile)

    blank = jnp.zeros((WIDTH - 6 * SUB, WIDTH), f32)
    depth = 6 * SUB

    def near_step(step, _):
        for k in range(4):
            block = step * 4 + k
            h, m, l = split_three(features(OWN, block, True))
            stack = jnp.concatenate([h, h, m, m, h, l, blank], axis=0)
            near_ref[block] = jnp.transpose(stack).astype(bf16)
        return 0

    lax.fori_loop(0, BLOCKS // 4, near_step, 0)

    pl.semaphore_wait(barrier, len(partners))
    first = [
        remote(pos_ref, first_ref.at[8 - c], first_send.at[c], first_recv.at[8 - c], tile_at(c))
        for c in sides
    ]
    for copy in first:
        copy.start()
    for copy in loads[1:]:
        copy.wait()

    def halo_copies(it, into):
        return [
            remote(
                basis_ref.at[it], into.at[8 - c],
                halo_send.at[it, c], halo_recv.at[it, 8 - c], tile_at(c),
            )
            for c in sides
        ]

    eye_b = lax.broadcasted_iota(jnp.int32, (BLOCKS, BLOCKS), 0) == lax.broadcasted_iota(
        jnp.int32, (BLOCKS, BLOCKS), 1
    )
    count = jnp.sum(
        jnp.where(eye_b, count_ref[...].astype(f32), 0.0), axis=1, keepdims=True
    )
    lanes = lax.broadcasted_iota(jnp.int32, (BLOCKS, WIDTH), 1).astype(f32)
    live = (lanes < count).astype(f32)
    noise = noise_ref[...]
    precond = 1.0 / (noise + signal_amp)
    right_side = live * delta_ref[...]
    image_ref[0] = right_side
    basis_ref[0] = precond * right_side

    halo_refs = (halo0_ref, halo1_ref, halo2_ref)
    halo0_ref[OWN] = basis_ref[0]

    shape = (slots, slots)
    rows_s = lax.broadcasted_iota(jnp.int32, shape, 0)
    lanes_s = lax.broadcasted_iota(jnp.int32, shape, 1)
    codes = pair_ref[0]
    near_row = (codes >= 3).astype(jnp.int32) + (codes >= 6).astype(jnp.int32)
    row_s = me_s + near_row - 1
    row_g = me_g + (codes - 3 * near_row) - 1
    filled = codes < CODES
    inside = filled & (row_s >= 0) & (row_s < n_sky) & (row_g >= 0) & (row_g < n_gz)
    target = pair_ref[2]
    target_col = jnp.sum(jnp.where(rows_s == lanes_s, target, 0), axis=1, keepdims=True)
    before = (target < target_col) | ((target == target_col) & (lanes_s < rows_s))
    rank = jnp.sum(before.astype(jnp.int32), axis=1, keepdims=True)
    place = rank == lanes_s
    fields = (jnp.minimum(codes, CODES - 1), pair_ref[1], target, inside.astype(jnp.int32))
    limits = (CODES - 1, BLOCKS - 1, BLOCKS - 1, 1)
    table = jnp.zeros((SUB, slots), jnp.int32)
    for i, (field, limit) in enumerate(zip(fields, limits)):
        column = jnp.sum(jnp.where(rows_s == lanes_s, field, 0), axis=1, keepdims=True)
        moved = jnp.sum(jnp.where(place, column, 0), axis=0, keepdims=True)
        table = jnp.where(sub == i, jnp.clip(moved, 0, limit), table)
    ends = jnp.sum((target_col <= lanes_s).astype(jnp.int32), axis=0, keepdims=True)
    table = jnp.where(sub == len(fields), jnp.clip(ends, 0, slots), table)
    order_ref[...] = table
    to_scalar = pltpu.make_async_copy(order_ref, spair_ref, load_sem.at[5])
    to_scalar.start()

    flat = table[0:1] * BLOCKS + table[1:2]
    weight = table[3:4].astype(f32) * signal_amp
    hits = lax.broadcasted_iota(jnp.int32, (BLOCKS, slots), 0) == target
    named = jnp.sum(
        jnp.where(hits & filled, signal_amp, 0.0), axis=1, keepdims=True
    )
    rows_f = lax.broadcasted_iota(jnp.int32, (CODES * BLOCKS, slots), 0)
    backs = jnp.where(rows_f == flat, weight, 0.0)
    from_ref[:, :slots] = backs.astype(bf16)
    from_ref[:, slots:] = backs.astype(bf16)
    source_col = jnp.sum(
        jnp.where(rows_s == lanes_s, table[1:2], 0), axis=1, keepdims=True
    )
    by_code = jnp.where(
        lax.broadcasted_iota(jnp.int32, (2 * SUB, slots), 0) == table[0:1], weight, 0.0
    )
    sourced = mm(by_code.astype(bf16), (source_col == lanes_s).astype(bf16))
    for c in range(CODES):
        owed_ref[0, c, BLOCKS:] = jnp.broadcast_to(sourced[c : c + 1], (SUB, WIDTH))

    def spread(values):
        for block in range(BLOCKS):
            column_ref[block] = jnp.transpose(
                jnp.broadcast_to(values[block : block + 1], (WIDTH, WIDTH))
            )

    spread(basis_ref[0])

    def make_tile(slot, block, code, source):
        h, m, l = split_three(features(code, source, False))
        stack = jnp.concatenate([h, m, h, m, l, h], axis=0).astype(bf16)
        cov_ref[slot] = jnp.exp2(mm(near_ref[block, :, :depth], stack))

    def self_tile(step, _):
        for k in range(4):
            block = step * 4 + k
            make_tile(slots + block, block, OWN, block)
        return 0

    lax.fori_loop(0, BLOCKS // 4, self_tile, 0)
    to_scalar.wait()
    for copy in first:
        copy.wait_recv()
    arriving = halo_copies(0, halo0_ref)
    for copy in arriving:
        copy.start()

    def down(slot, block):
        product = cov_ref[slot] * column_ref[block]
        return jnp.sum(
            jnp.sum(product.reshape(WIDTH // SUB, SUB, WIDTH), axis=0), axis=0, keepdims=True
        )

    def doubled(values):
        high, low = split_two(values)
        return jnp.concatenate([high, low], axis=0)

    lanes_sq = lax.broadcasted_iota(jnp.int32, (WIDTH, WIDTH), 1)
    ones = jnp.ones((2 * WIDTH, WIDTH), bf16)
    in_flight = first
    own_weight = None
    for it in range(ITERS):
        vector = basis_ref[it]
        halo_ref = halo_refs[it]
        if it > 0:
            arriving = halo_copies(it, halo_ref)
            for copy in arriving:
                copy.start()
            halo_ref[OWN] = vector

        if it > 0:
            spread(vector)

        if it == 0:

            def pair_tile(step, _):
                for k in range(32):
                    slot = step * 32 + k
                    make_tile(slot, spair_ref[2, slot], spair_ref[0, slot], spair_ref[1, slot])
                return 0

            lax.fori_loop(0, slots // 32, pair_tile, 0)

        def pay_step(step, _):
            total = jnp.zeros((SUB, WIDTH), f32)
            for k in range(SUB):
                slot = step * SUB + k
                total = jnp.where(sub == k, down(slot, spair_ref[2, slot]), total)
            pay_ref[pl.ds(step * SUB, SUB), :] = total
            return 0

        lax.fori_loop(0, slots // SUB, pay_step, 0)
        pays = doubled(pay_ref[...])
        extent = BLOCKS + SUB if it == 0 else BLOCKS
        returns = [
            remote(
                owed_ref.at[it, c, pl.ds(0, extent)], got_ref.at[it, 8 - c, pl.ds(0, extent)],
                owed_send.at[it, c], owed_recv.at[it, 8 - c], tile_at(c),
            )
            for c in sides
        ]
        for copy, c in zip(returns, sides):
            owed_ref[it, c, 0:BLOCKS] = mm(from_ref[c * BLOCKS : (c + 1) * BLOCKS], pays)
            copy.start()
        owed_ref[it, OWN, 0:BLOCKS] = mm(from_ref[OWN * BLOCKS : (OWN + 1) * BLOCKS], pays)

        def self_step(step, _):
            total = jnp.zeros((SUB, WIDTH), f32)
            for k in range(SUB):
                block = step * SUB + k
                total = jnp.where(sub == k, down(slots + block, block), total)
            self_ref[pl.ds(step * SUB, SUB), :] = total
            return 0

        lax.fori_loop(0, BLOCKS // SUB, self_step, 0)
        for copy in arriving:
            copy.wait_recv()

        def gain_step(step, running):
            for k in range(2 * SUB):
                slot = step * 2 * SUB + k
                row = halo_ref[spair_ref[0, slot], pl.ds(spair_ref[1, slot], 1), :]
                row = row * (spair_ref[3, slot].astype(f32) * signal_amp)
                same = spair_ref[2, slot] == spair_ref[2, jnp.maximum(slot - 1, 0)]
                running = running * same.astype(f32) + cov_ref[slot] * row
                running_ref[slot] = running
            return running

        lax.fori_loop(0, slots // SUB // 2, gain_step, jnp.zeros((WIDTH, WIDTH), f32))
        tall = jnp.zeros((WIDTH, WIDTH), f32)
        for block in range(BLOCKS):
            end = spair_ref[4, block]
            start = spair_ref[4, block - 1] if block > 0 else 0
            sums = running_ref[jnp.clip(end - 1, 0, slots - 1)]
            if block % 2 == 0:
                high, low = split_two(sums)
                reach = mm(jnp.concatenate([high, low], axis=1), ones)
            else:
                reach = jnp.sum(sums, axis=1, keepdims=True)
            reach = reach * (end > start).astype(f32)
            tall = jnp.where(lanes_sq == block, reach, tall)
        totals = jnp.transpose(tall)[:BLOCKS]
        totals = totals + owed_ref[it, OWN, 0:BLOCKS]
        for copy in returns:
            copy.wait_recv()
        for c in sides:
            totals = totals + got_ref[it, c, 0:BLOCKS]
        if it == 0:
            sources = owed_ref[0, OWN, BLOCKS:]
            for c in sides:
                sources = sources + got_ref[0, c, BLOCKS:]
            own_lane = lax.broadcasted_iota(
                jnp.int32, (BLOCKS, WIDTH), 0
            ) == lax.broadcasted_iota(jnp.int32, (BLOCKS, WIDTH), 1)
            own_weight = signal_amp + named + jnp.sum(
                jnp.where(own_lane, sources[0:1], 0.0), axis=1, keepdims=True
            )
        totals = totals + own_weight * self_ref[...]
        image = live * totals + noise * vector
        image_ref[it + 1] = image
        basis_ref[it + 1] = precond * image
        in_flight = in_flight + arriving + returns

    moments = jnp.zeros((SUB, WIDTH), f32)
    for m in range(2 * ITERS + 1):
        product = basis_ref[m // 2] * image_ref[m - m // 2]
        moments = jnp.where(sub == m, jnp.sum(product, axis=0, keepdims=True), moments)
    stages = (
        (gz_at, n_gz, red1_ref, red1_send, red1_recv),
        (inner_at, INNER, red2_ref, red2_send, red2_recv),
        (outer_at, n_outer, red3_ref, red3_send, red3_recv),
    )
    for stage, (device_at, members, into, send, recv) in enumerate(stages):
        sum_ref[stage] = moments
        copies = [
            remote(
                sum_ref.at[stage], into.at[step - 1], send.at[step - 1], recv.at[step - 1],
                device_at(step),
            )
            for step in range(1, members)
        ]
        for copy in copies:
            copy.start()
        for copy in in_flight:
            copy.wait_send()
        in_flight = copies
        for step, copy in enumerate(copies):
            copy.wait_recv()
            moments = moments + into[step]
    total = jnp.sum(moments, axis=1, keepdims=True)
    mu = [total[m : m + 1] for m in range(2 * ITERS + 1)]

    def inner_product(left, right):
        value = None
        for i, a in enumerate(left):
            for j, b in enumerate(right):
                if a is not None and b is not None:
                    term = a * b * mu[i + j]
                    value = term if value is None else value + term
        return value

    def plus(left, scale, right):
        if right is None:
            return left
        return scale * right if left is None else left + scale * right

    one = jnp.ones((1, 1), f32)
    resid = [one, None, None, None]
    direct = [one, None, None, None]
    field = [None, None, None, None]
    rz = mu[0]
    for it in range(ITERS):
        moved = [None] + direct[:-1]
        alpha = rz / inner_product(direct, moved)
        field = [plus(a, alpha, b) for a, b in zip(field, direct)]
        resid = [plus(a, -alpha, b) for a, b in zip(resid, moved)]
        if it + 1 < ITERS:
            new = inner_product(resid, resid)
            beta = new / rz
            direct = [plus(a, beta, b) for a, b in zip(resid, direct)]
            rz = new
    out_field = field[0] * basis_ref[0]
    for i in range(1, ITERS):
        out_field = out_field + field[i] * basis_ref[i]
    out_resid = image_ref[0]
    for i in range(1, ITERS + 1):
        out_resid = out_resid + resid[i] * image_ref[i]
    out_ref[0] = out_field
    out_ref[1] = out_resid
    for copy in in_flight:
        copy.wait_send()


def local(delta_flux, noise_var, pixel_pos, pixel_count, pair_list):
    slots = pair_list.shape[3]
    n_sky = lax.axis_size("sky")
    n_gz = lax.axis_size("gz")
    n_outer = n_sky // INNER
    vmem = pl.BlockSpec(memory_space=pltpu.VMEM)
    hbm = pl.BlockSpec(memory_space=pltpu.HBM)
    shape = jax.ShapeDtypeStruct((2, BLOCKS, WIDTH), f32)
    dma = pltpu.SemaphoreType.DMA
    both = pl.pallas_call(
        functools.partial(body, slots),
        out_shape=shape,
        in_specs=[hbm] * 5,
        out_specs=vmem,
        scratch_shapes=[
            pltpu.VMEM((BLOCKS, WIDTH), f32),
            pltpu.VMEM((BLOCKS, WIDTH), f32),
            pltpu.VMEM((3, BLOCKS, WIDTH), f32),
            pltpu.VMEM((1, BLOCKS), jnp.int32),
            pltpu.VMEM((3, 1, slots), jnp.int32),
            pltpu.VMEM((SUB, slots), jnp.int32),
            pltpu.SMEM((SUB, slots), jnp.int32),
            pltpu.VMEM((BLOCKS, WIDTH, WIDTH), bf16),
            pltpu.VMEM((slots + BLOCKS, WIDTH, WIDTH), f32),
            pltpu.VMEM((slots, WIDTH, WIDTH), f32),
            pltpu.VMEM((BLOCKS, WIDTH, WIDTH), f32),
            pltpu.VMEM((CODES, 3, BLOCKS, WIDTH), f32),
            pltpu.VMEM((CODES, BLOCKS, WIDTH), f32),
            pltpu.VMEM((CODES, BLOCKS, WIDTH), f32),
            pltpu.VMEM((CODES, BLOCKS, WIDTH), f32),
            pltpu.VMEM((ITERS, CODES, BLOCKS + SUB, WIDTH), f32),
            pltpu.VMEM((ITERS, CODES, BLOCKS + SUB, WIDTH), f32),
            pltpu.VMEM((slots, WIDTH), f32),
            pltpu.VMEM((BLOCKS, WIDTH), f32),
            pltpu.VMEM((ITERS + 1, BLOCKS, WIDTH), f32),
            pltpu.VMEM((ITERS + 1, BLOCKS, WIDTH), f32),
            pltpu.VMEM((CODES * BLOCKS, 2 * slots), bf16),
            pltpu.VMEM((3, SUB, WIDTH), f32),
            pltpu.VMEM((n_gz - 1, SUB, WIDTH), f32),
            pltpu.VMEM((INNER - 1, SUB, WIDTH), f32),
            pltpu.VMEM((n_outer - 1, SUB, WIDTH), f32),
            dma((6,)), dma((CODES,)), dma((CODES,)),
            dma((ITERS, CODES)), dma((ITERS, CODES)),
            dma((ITERS, CODES)), dma((ITERS, CODES)),
            dma((n_gz - 1,)), dma((n_gz - 1,)),
            dma((INNER - 1,)), dma((INNER - 1,)),
            dma((n_outer - 1,)), dma((n_outer - 1,)),
        ],
        compiler_params=pltpu.CompilerParams(
            collective_id=0, has_side_effects=True, vmem_limit_bytes=40 * 1024 * 1024
        ),
    )(
        *(
            pltpu.with_memory_space_constraint(value, pltpu.HBM)
            for value in (
                delta_flux, noise_var, pixel_pos, pixel_count, jnp.transpose(pair_list, (0, 2, 1, 3))
            )
        )
    )
    return both[0][None, None], both[1][None, None]


def solution(mesh):
    placed = (
        P("sky", "gz", None, None),
        P("sky", "gz", None, None),
        P("sky", "gz", None, None, None),
        P("sky", "gz", None),
        P("sky", "gz", None, None),
    )
    return jax.shard_map(
        local,
        mesh=mesh,
        in_specs=placed,
        out_specs=(P("sky", "gz", None, None), P("sky", "gz", None, None)),
        check_vma=False,
    )
```

```python
import functools
import math
import jax
import jax.numpy as jnp
from jax import lax
from jax.experimental import pallas as pl
from jax.experimental.pallas import tpu as pltpu
from jax.sharding import PartitionSpec as P

ITERS = 3
BLOCKS = 32
WIDTH = 128
CODES = 9
OWN = 4
SUB = 8
INNER = 8

signal_amp = 0.25
bf16 = jnp.bfloat16
f32 = jnp.float32


def mm(left, right):
    return lax.dot_general(left, right, (((1,), (0,)), ((), ())), preferred_element_type=f32)


def mm_trans(left, right):
    return lax.dot_general(left, right, (((1,), (1,)), ((), ())), preferred_element_type=f32)


def split_two(values):
    high = values.astype(bf16)
    return high, (values - high.astype(f32)).astype(bf16)


def split_three(values):
    high = values.astype(bf16).astype(f32)
    rest = values - high
    mid = rest.astype(bf16).astype(f32)
    return high, mid, rest - mid


def body(
    slots,
    delta_in, noise_in, pos_in, count_in, pair_in,
    out_ref,
    delta_ref, noise_ref, pos_ref, count_ref, pair_ref, order_ref, spair_ref,
    near_ref, cov_ref, running_ref, column_ref, first_ref, halo0_ref, halo1_ref, halo2_ref, owed_ref, got_ref,
    pay_ref, self_ref, basis_ref, image_ref, from_ref,
    sum_ref, red1_ref, red2_ref, red3_ref,
    load_sem, first_send, first_recv, halo_send, halo_recv, owed_send, owed_recv,
    red1_send, red1_recv, red2_send, red2_recv, red3_send, red3_recv,
):
    n_sky = lax.axis_size("sky")
    n_gz = lax.axis_size("gz")
    n_outer = n_sky // INNER
    me_s = lax.axis_index("sky")
    me_g = lax.axis_index("gz")
    outer = me_s // INNER
    inner = me_s % INNER

    def tile_at(code):
        return (
            (me_s + code // 3 - 1 + n_sky) % n_sky,
            (me_g + code % 3 - 1 + n_gz) % n_gz,
        )

    def gz_at(step):
        return (me_s, (me_g + step) % n_gz)

    def inner_at(step):
        return (outer * INNER + (inner + step) % INNER, me_g)

    def outer_at(step):
        return ((outer + step) % n_outer * INNER + inner, me_g)

    sides = (0, 2, 6, 8, 1, 7, 3, 5)
    partners = [tile_at(code) for code in sides]
    partners += [gz_at(step) for step in range(2, n_gz - 1)]
    partners += [inner_at(step) for step in range(1, INNER)]
    partners += [outer_at(step) for step in range(1, n_outer)]
    loads = [
        pltpu.make_async_copy(source, into, load_sem.at[i])
        for i, (source, into) in enumerate(
            (
                (pos_in.at[0, 0], pos_ref),
                (pair_in.at[0], pair_ref),
                (count_in.at[0], count_ref),
                (noise_in.at[0, 0], noise_ref),
                (delta_in.at[0, 0], delta_ref),
            )
        )
    ]
    for copy in loads:
        copy.start()
    barrier = pltpu.get_barrier_semaphore()
    for partner in partners:
        pl.semaphore_signal(
            barrier, inc=1, device_id=partner, device_id_type=pl.DeviceIdType.MESH
        )

    def remote(source, target, send, recv, device):
        return pltpu.make_async_remote_copy(
            src_ref=source, dst_ref=target, send_sem=send, recv_sem=recv,
            device_id=device, device_id_type=pl.DeviceIdType.MESH,
        )

    loads[0].wait()
    first_ref[OWN] = pos_ref[...]

    sub = lax.broadcasted_iota(jnp.int32, (SUB, WIDTH), 0)
    mid_x = (2 * me_s + 1).astype(f32)
    mid_z = (4 * me_g + 2).astype(f32)
    scale = math.sqrt(math.log2(math.e))
    def features(code, block, swap):
        x = (first_ref[code, 0, pl.ds(block, 1), :] - mid_x) * scale
        y = (first_ref[code, 1, pl.ds(block, 1), :] - 1.0) * scale
        z = (first_ref[code, 2, pl.ds(block, 1), :] - mid_z) * scale
        size = -0.5 * (x * x + y * y + z * z)
        tile = jnp.where(sub == 0, x, 0.0)
        tile = jnp.where(sub == 1, y, tile)
        tile = jnp.where(sub == 2, z, tile)
        tile = jnp.where(sub == (3 if swap else 4), size, tile)
        return jnp.where(sub == (4 if swap else 3), 1.0, tile)

    blank = jnp.zeros((WIDTH - 6 * SUB, WIDTH), f32)
    depth = 6 * SUB

    def near_step(step, _):
        for k in range(4):
            block = step * 4 + k
            h, m, l = split_three(features(OWN, block, True))
            stack = jnp.concatenate([h, h, m, m, h, l, blank], axis=0)
            near_ref[block] = jnp.transpose(stack).astype(bf16)
        return 0

    lax.fori_loop(0, BLOCKS // 4, near_step, 0)

    pl.semaphore_wait(barrier, len(partners))
    first = [
        remote(pos_ref, first_ref.at[8 - c], first_send.at[c], first_recv.at[8 - c], tile_at(c))
        for c in sides
    ]
    for copy in first:
        copy.start()
    for copy in loads[1:]:
        copy.wait()

    def halo_copies(it, into):
        return [
            remote(
                basis_ref.at[it], into.at[8 - c],
                halo_send.at[it, c], halo_recv.at[it, 8 - c], tile_at(c),
            )
            for c in sides
        ]

    eye_b = lax.broadcasted_iota(jnp.int32, (BLOCKS, BLOCKS), 0) == lax.broadcasted_iota(
        jnp.int32, (BLOCKS, BLOCKS), 1
    )
    count = jnp.sum(
        jnp.where(eye_b, count_ref[...].astype(f32), 0.0), axis=1, keepdims=True
    )
    lanes = lax.broadcasted_iota(jnp.int32, (BLOCKS, WIDTH), 1).astype(f32)
    live = (lanes < count).astype(f32)
    noise = noise_ref[...]
    precond = 1.0 / (noise + signal_amp)
    right_side = live * delta_ref[...]
    image_ref[0] = right_side
    basis_ref[0] = precond * right_side

    halo_refs = (halo0_ref, halo1_ref, halo2_ref)
    halo0_ref[OWN] = basis_ref[0]

    shape = (slots, slots)
    rows_s = lax.broadcasted_iota(jnp.int32, shape, 0)
    lanes_s = lax.broadcasted_iota(jnp.int32, shape, 1)
    codes = pair_ref[0]
    near_row = (codes >= 3).astype(jnp.int32) + (codes >= 6).astype(jnp.int32)
    row_s = me_s + near_row - 1
    row_g = me_g + (codes - 3 * near_row) - 1
    filled = codes < CODES
    inside = filled & (row_s >= 0) & (row_s < n_sky) & (row_g >= 0) & (row_g < n_gz)
    target = pair_ref[2]
    target_col = jnp.sum(jnp.where(rows_s == lanes_s, target, 0), axis=1, keepdims=True)
    before = (target < target_col) | ((target == target_col) & (lanes_s < rows_s))
    rank = jnp.sum(before.astype(jnp.int32), axis=1, keepdims=True)
    place = rank == lanes_s
    fields = (jnp.minimum(codes, CODES - 1), pair_ref[1], target, inside.astype(jnp.int32))
    limits = (CODES - 1, BLOCKS - 1, BLOCKS - 1, 1)
    table = jnp.zeros((SUB, slots), jnp.int32)
    for i, (field, limit) in enumerate(zip(fields, limits)):
        column = jnp.sum(jnp.where(rows_s == lanes_s, field, 0), axis=1, keepdims=True)
        moved = jnp.sum(jnp.where(place, column, 0), axis=0, keepdims=True)
        table = jnp.where(sub == i, jnp.clip(moved, 0, limit), table)
    ends = jnp.sum((target_col <= lanes_s).astype(jnp.int32), axis=0, keepdims=True)
    table = jnp.where(sub == len(fields), jnp.clip(ends, 0, slots), table)
    order_ref[...] = table
    to_scalar = pltpu.make_async_copy(order_ref, spair_ref, load_sem.at[5])
    to_scalar.start()

    flat = table[0:1] * BLOCKS + table[1:2]
    weight = table[3:4].astype(f32) * signal_amp
    hits = lax.broadcasted_iota(jnp.int32, (BLOCKS, slots), 0) == target
    named = jnp.sum(
        jnp.where(hits & filled, signal_amp, 0.0), axis=1, keepdims=True
    )
    rows_f = lax.broadcasted_iota(jnp.int32, (CODES * BLOCKS, slots), 0)
    backs = jnp.where(rows_f == flat, weight, 0.0)
    from_ref[:, :slots] = backs.astype(bf16)
    from_ref[:, slots:] = backs.astype(bf16)
    source_col = jnp.sum(
        jnp.where(rows_s == lanes_s, table[1:2], 0), axis=1, keepdims=True
    )
    by_code = jnp.where(
        lax.broadcasted_iota(jnp.int32, (2 * SUB, slots), 0) == table[0:1], weight, 0.0
    )
    sourced = mm(by_code.astype(bf16), (source_col == lanes_s).astype(bf16))
    for c in range(CODES):
        owed_ref[0, c, BLOCKS:] = jnp.broadcast_to(sourced[c : c + 1], (SUB, WIDTH))

    def spread(values):
        for block in range(BLOCKS):
            column_ref[block] = jnp.transpose(
                jnp.broadcast_to(values[block : block + 1], (WIDTH, WIDTH))
            )

    spread(basis_ref[0])

    def make_tile(slot, block, code, source):
        h, m, l = split_three(features(code, source, False))
        stack = jnp.concatenate([h, m, h, m, l, h], axis=0).astype(bf16)
        cov_ref[slot] = jnp.exp2(mm(near_ref[block, :, :depth], stack))

    def self_tile(step, _):
        for k in range(4):
            block = step * 4 + k
            make_tile(slots + block, block, OWN, block)
        return 0

    lax.fori_loop(0, BLOCKS // 4, self_tile, 0)
    to_scalar.wait()
    for copy in first:
        copy.wait_recv()
    arriving = halo_copies(0, halo0_ref)
    for copy in arriving:
        copy.start()

    def down(slot, block):
        product = cov_ref[slot] * column_ref[block]
        return jnp.sum(
            jnp.sum(product.reshape(WIDTH // SUB, SUB, WIDTH), axis=0), axis=0, keepdims=True
        )

    def doubled(values):
        high, low = split_two(values)
        return jnp.concatenate([high, low], axis=0)

    lanes_sq = lax.broadcasted_iota(jnp.int32, (WIDTH, WIDTH), 1)
    ones = jnp.ones((2 * WIDTH, WIDTH), bf16)
    def with_moment(moments, m):
        product = basis_ref[m // 2] * image_ref[m - m // 2]
        return jnp.where(sub == m, jnp.sum(product, axis=0, keepdims=True), moments)

    in_flight = first
    own_weight = None
    for it in range(ITERS):
        vector = basis_ref[it]
        halo_ref = halo_refs[it]
        if it > 0:
            arriving = halo_copies(it, halo_ref)
            for copy in arriving:
                copy.start()
            halo_ref[OWN] = vector

        if it > 0:
            spread(vector)

        if it == 0:

            def pair_tile(step, _):
                for k in range(64):
                    slot = step * 64 + k
                    make_tile(slot, spair_ref[2, slot], spair_ref[0, slot], spair_ref[1, slot])
                return 0

            lax.fori_loop(0, slots // 64, pair_tile, 0)

        def pay_step(step, _):
            total = jnp.zeros((SUB, WIDTH), f32)
            for k in range(SUB):
                slot = step * SUB + k
                total = jnp.where(sub == k, down(slot, spair_ref[2, slot]), total)
            pay_ref[pl.ds(step * SUB, SUB), :] = total
            return 0

        lax.fori_loop(0, slots // SUB, pay_step, 0)
        pays = doubled(pay_ref[...])
        extent = BLOCKS + SUB if it == 0 else BLOCKS
        returns = [
            remote(
                owed_ref.at[it, c, pl.ds(0, extent)], got_ref.at[it, 8 - c, pl.ds(0, extent)],
                owed_send.at[it, c], owed_recv.at[it, 8 - c], tile_at(c),
            )
            for c in sides
        ]
        for copy, c in zip(returns, sides):
            owed_ref[it, c, 0:BLOCKS] = mm(from_ref[c * BLOCKS : (c + 1) * BLOCKS], pays)
            copy.start()
        owed_ref[it, OWN, 0:BLOCKS] = mm(from_ref[OWN * BLOCKS : (OWN + 1) * BLOCKS], pays)

        def self_step(step, _):
            total = jnp.zeros((SUB, WIDTH), f32)
            for k in range(SUB):
                block = step * SUB + k
                total = jnp.where(sub == k, down(slots + block, block), total)
            self_ref[pl.ds(step * SUB, SUB), :] = total
            return 0

        lax.fori_loop(0, BLOCKS // SUB, self_step, 0)
        for copy in arriving:
            copy.wait_recv()

        def gain_step(step, running):
            for k in range(2 * SUB):
                slot = step * 2 * SUB + k
                row = halo_ref[spair_ref[0, slot], pl.ds(spair_ref[1, slot], 1), :]
                row = row * (spair_ref[3, slot].astype(f32) * signal_amp)
                same = spair_ref[2, slot] == spair_ref[2, jnp.maximum(slot - 1, 0)]
                running = running * same.astype(f32) + cov_ref[slot] * row
                running_ref[slot] = running
            return running

        lax.fori_loop(0, slots // SUB // 2, gain_step, jnp.zeros((WIDTH, WIDTH), f32))
        tall = jnp.zeros((WIDTH, WIDTH), f32)
        for block in range(BLOCKS):
            end = spair_ref[4, block]
            start = spair_ref[4, block - 1] if block > 0 else 0
            sums = running_ref[jnp.clip(end - 1, 0, slots - 1)]
            if block % 2 == 0:
                high, low = split_two(sums)
                reach = mm(jnp.concatenate([high, low], axis=1), ones)
            else:
                reach = jnp.sum(sums, axis=1, keepdims=True)
            reach = reach * (end > start).astype(f32)
            tall = jnp.where(lanes_sq == block, reach, tall)
        totals = jnp.transpose(tall)[:BLOCKS]
        totals = totals + owed_ref[it, OWN, 0:BLOCKS]
        if it == ITERS - 1:
            moments = jnp.zeros((SUB, WIDTH), f32)
            for m in range(2 * ITERS - 1):
                moments = with_moment(moments, m)
        for copy in returns:
            copy.wait_recv()
        for c in sides:
            totals = totals + got_ref[it, c, 0:BLOCKS]
        if it == 0:
            sources = owed_ref[0, OWN, BLOCKS:]
            for c in sides:
                sources = sources + got_ref[0, c, BLOCKS:]
            own_lane = lax.broadcasted_iota(
                jnp.int32, (BLOCKS, WIDTH), 0
            ) == lax.broadcasted_iota(jnp.int32, (BLOCKS, WIDTH), 1)
            own_weight = signal_amp + named + jnp.sum(
                jnp.where(own_lane, sources[0:1], 0.0), axis=1, keepdims=True
            )
        totals = totals + own_weight * self_ref[...]
        image = live * totals + noise * vector
        image_ref[it + 1] = image
        basis_ref[it + 1] = precond * image
        in_flight = in_flight + arriving + returns

    for m in range(2 * ITERS - 1, 2 * ITERS + 1):
        moments = with_moment(moments, m)
    stages = (
        (gz_at, n_gz, red1_ref, red1_send, red1_recv),
        (inner_at, INNER, red2_ref, red2_send, red2_recv),
        (outer_at, n_outer, red3_ref, red3_send, red3_recv),
    )
    for stage, (device_at, members, into, send, recv) in enumerate(stages):
        sum_ref[stage] = moments
        copies = [
            remote(
                sum_ref.at[stage], into.at[step - 1], send.at[step - 1], recv.at[step - 1],
                device_at(step),
            )
            for step in range(1, members)
        ]
        for copy in copies:
            copy.start()
        for copy in in_flight:
            copy.wait_send()
        in_flight = copies
        for step, copy in enumerate(copies):
            copy.wait_recv()
            moments = moments + into[step]
    total = jnp.sum(moments, axis=1, keepdims=True)
    mu = [total[m : m + 1] for m in range(2 * ITERS + 1)]

    def inner_product(left, right):
        value = None
        for i, a in enumerate(left):
            for j, b in enumerate(right):
                if a is not None and b is not None:
                    term = a * b * mu[i + j]
                    value = term if value is None else value + term
        return value

    def plus(left, scale, right):
        if right is None:
            return left
        return scale * right if left is None else left + scale * right

    one = jnp.ones((1, 1), f32)
    resid = [one, None, None, None]
    direct = [one, None, None, None]
    field = [None, None, None, None]
    rz = mu[0]
    for it in range(ITERS):
        moved = [None] + direct[:-1]
        alpha = rz / inner_product(direct, moved)
        field = [plus(a, alpha, b) for a, b in zip(field, direct)]
        resid = [plus(a, -alpha, b) for a, b in zip(resid, moved)]
        if it + 1 < ITERS:
            new = inner_product(resid, resid)
            beta = new / rz
            direct = [plus(a, beta, b) for a, b in zip(resid, direct)]
            rz = new
    out_field = field[0] * basis_ref[0]
    for i in range(1, ITERS):
        out_field = out_field + field[i] * basis_ref[i]
    out_resid = image_ref[0]
    for i in range(1, ITERS + 1):
        out_resid = out_resid + resid[i] * image_ref[i]
    out_ref[0] = out_field
    out_ref[1] = out_resid
    for copy in in_flight:
        copy.wait_send()


def local(delta_flux, noise_var, pixel_pos, pixel_count, pair_list):
    slots = pair_list.shape[3]
    n_sky = lax.axis_size("sky")
    n_gz = lax.axis_size("gz")
    n_outer = n_sky // INNER
    vmem = pl.BlockSpec(memory_space=pltpu.VMEM)
    hbm = pl.BlockSpec(memory_space=pltpu.HBM)
    shape = jax.ShapeDtypeStruct((2, BLOCKS, WIDTH), f32)
    dma = pltpu.SemaphoreType.DMA
    both = pl.pallas_call(
        functools.partial(body, slots),
        out_shape=shape,
        in_specs=[hbm] * 5,
        out_specs=vmem,
        scratch_shapes=[
            pltpu.VMEM((BLOCKS, WIDTH), f32),
            pltpu.VMEM((BLOCKS, WIDTH), f32),
            pltpu.VMEM((3, BLOCKS, WIDTH), f32),
            pltpu.VMEM((1, BLOCKS), jnp.int32),
            pltpu.VMEM((3, 1, slots), jnp.int32),
            pltpu.VMEM((SUB, slots), jnp.int32),
            pltpu.SMEM((SUB, slots), jnp.int32),
            pltpu.VMEM((BLOCKS, WIDTH, WIDTH), bf16),
            pltpu.VMEM((slots + BLOCKS, WIDTH, WIDTH), f32),
            pltpu.VMEM((slots, WIDTH, WIDTH), f32),
            pltpu.VMEM((BLOCKS, WIDTH, WIDTH), f32),
            pltpu.VMEM((CODES, 3, BLOCKS, WIDTH), f32),
            pltpu.VMEM((CODES, BLOCKS, WIDTH), f32),
            pltpu.VMEM((CODES, BLOCKS, WIDTH), f32),
            pltpu.VMEM((CODES, BLOCKS, WIDTH), f32),
            pltpu.VMEM((ITERS, CODES, BLOCKS + SUB, WIDTH), f32),
            pltpu.VMEM((ITERS, CODES, BLOCKS + SUB, WIDTH), f32),
            pltpu.VMEM((slots, WIDTH), f32),
            pltpu.VMEM((BLOCKS, WIDTH), f32),
            pltpu.VMEM((ITERS + 1, BLOCKS, WIDTH), f32),
            pltpu.VMEM((ITERS + 1, BLOCKS, WIDTH), f32),
            pltpu.VMEM((CODES * BLOCKS, 2 * slots), bf16),
            pltpu.VMEM((3, SUB, WIDTH), f32),
            pltpu.VMEM((n_gz - 1, SUB, WIDTH), f32),
            pltpu.VMEM((INNER - 1, SUB, WIDTH), f32),
            pltpu.VMEM((n_outer - 1, SUB, WIDTH), f32),
            dma((6,)), dma((CODES,)), dma((CODES,)),
            dma((ITERS, CODES)), dma((ITERS, CODES)),
            dma((ITERS, CODES)), dma((ITERS, CODES)),
            dma((n_gz - 1,)), dma((n_gz - 1,)),
            dma((INNER - 1,)), dma((INNER - 1,)),
            dma((n_outer - 1,)), dma((n_outer - 1,)),
        ],
        compiler_params=pltpu.CompilerParams(
            collective_id=0, has_side_effects=True, vmem_limit_bytes=40 * 1024 * 1024
        ),
    )(
        *(
            pltpu.with_memory_space_constraint(value, pltpu.HBM)
            for value in (
                delta_flux, noise_var, pixel_pos, pixel_count, jnp.transpose(pair_list, (0, 2, 1, 3))
            )
        )
    )
    return both[0][None, None], both[1][None, None]


def solution(mesh):
    placed = (
        P("sky", "gz", None, None),
        P("sky", "gz", None, None),
        P("sky", "gz", None, None, None),
        P("sky", "gz", None),
        P("sky", "gz", None, None),
    )
    return jax.shard_map(
        local,
        mesh=mesh,
        in_specs=placed,
        out_specs=(P("sky", "gz", None, None), P("sky", "gz", None, None)),
        check_vma=False,
    )
```

```python
import functools
import math
import jax
import jax.numpy as jnp
from jax import lax
from jax.experimental import pallas as pl
from jax.experimental.pallas import tpu as pltpu
from jax.sharding import PartitionSpec as P

ITERS = 3
BLOCKS = 32
WIDTH = 128
CODES = 9
OWN = 4
SUB = 8
INNER = 8

signal_amp = 0.25
bf16 = jnp.bfloat16
f32 = jnp.float32


def mm(left, right):
    return lax.dot_general(left, right, (((1,), (0,)), ((), ())), preferred_element_type=f32)


def mm_trans(left, right):
    return lax.dot_general(left, right, (((1,), (1,)), ((), ())), preferred_element_type=f32)


def split_two(values):
    high = values.astype(bf16)
    return high, (values - high.astype(f32)).astype(bf16)


def split_three(values):
    high = values.astype(bf16).astype(f32)
    rest = values - high
    mid = rest.astype(bf16).astype(f32)
    return high, mid, rest - mid


def body(
    slots,
    delta_in, noise_in, pos_in, count_in, pair_in,
    out_ref,
    delta_ref, noise_ref, pos_ref, count_ref, pair_ref, order_ref, spair_ref,
    near_ref, cov_ref, running_ref, column_ref, first_ref, halo0_ref, halo1_ref, halo2_ref, owed_ref, got_ref,
    pay_ref, self_ref, basis_ref, image_ref, from_ref,
    sum_ref, red1_ref, red2_ref, red3_ref,
    load_sem, first_send, first_recv, halo_send, halo_recv, owed_send, owed_recv,
    red1_send, red1_recv, red2_send, red2_recv, red3_send, red3_recv,
):
    n_sky = lax.axis_size("sky")
    n_gz = lax.axis_size("gz")
    n_outer = n_sky // INNER
    me_s = lax.axis_index("sky")
    me_g = lax.axis_index("gz")
    outer = me_s // INNER
    inner = me_s % INNER

    def tile_at(code):
        return (
            (me_s + code // 3 - 1 + n_sky) % n_sky,
            (me_g + code % 3 - 1 + n_gz) % n_gz,
        )

    def gz_at(step):
        return (me_s, (me_g + step) % n_gz)

    def inner_at(step):
        return (outer * INNER + (inner + step) % INNER, me_g)

    def outer_at(step):
        return ((outer + step) % n_outer * INNER + inner, me_g)

    sides = (0, 2, 6, 8, 1, 7, 3, 5)
    partners = [tile_at(code) for code in sides]
    partners += [gz_at(step) for step in range(2, n_gz - 1)]
    partners += [inner_at(step) for step in range(1, INNER)]
    partners += [outer_at(step) for step in range(1, n_outer)]
    loads = [
        pltpu.make_async_copy(source, into, load_sem.at[i])
        for i, (source, into) in enumerate(
            (
                (pos_in.at[0, 0], pos_ref),
                (pair_in.at[0], pair_ref),
                (count_in.at[0], count_ref),
                (noise_in.at[0, 0], noise_ref),
                (delta_in.at[0, 0], delta_ref),
            )
        )
    ]
    for copy in loads:
        copy.start()
    barrier = pltpu.get_barrier_semaphore()
    for partner in partners:
        pl.semaphore_signal(
            barrier, inc=1, device_id=partner, device_id_type=pl.DeviceIdType.MESH
        )

    def remote(source, target, send, recv, device):
        return pltpu.make_async_remote_copy(
            src_ref=source, dst_ref=target, send_sem=send, recv_sem=recv,
            device_id=device, device_id_type=pl.DeviceIdType.MESH,
        )

    loads[0].wait()
    first_ref[OWN] = pos_ref[...]

    sub = lax.broadcasted_iota(jnp.int32, (SUB, WIDTH), 0)
    mid_x = (2 * me_s + 1).astype(f32)
    mid_z = (4 * me_g + 2).astype(f32)
    scale = math.sqrt(math.log2(math.e))
    def features(code, block, swap):
        x = (first_ref[code, 0, pl.ds(block, 1), :] - mid_x) * scale
        y = (first_ref[code, 1, pl.ds(block, 1), :] - 1.0) * scale
        z = (first_ref[code, 2, pl.ds(block, 1), :] - mid_z) * scale
        size = -0.5 * (x * x + y * y + z * z)
        tile = jnp.where(sub == 0, x, 0.0)
        tile = jnp.where(sub == 1, y, tile)
        tile = jnp.where(sub == 2, z, tile)
        tile = jnp.where(sub == (3 if swap else 4), size, tile)
        return jnp.where(sub == (4 if swap else 3), 1.0, tile)

    blank = jnp.zeros((WIDTH - 6 * SUB, WIDTH), f32)
    depth = 6 * SUB

    def near_step(step, _):
        for k in range(4):
            block = step * 4 + k
            h, m, l = split_three(features(OWN, block, True))
            stack = jnp.concatenate([h, h, m, m, h, l, blank], axis=0)
            near_ref[block] = jnp.transpose(stack).astype(bf16)
        return 0

    lax.fori_loop(0, BLOCKS // 4, near_step, 0)

    pl.semaphore_wait(barrier, len(partners))
    first = [
        remote(pos_ref, first_ref.at[8 - c], first_send.at[c], first_recv.at[8 - c], tile_at(c))
        for c in sides
    ]
    for copy in first:
        copy.start()
    for copy in loads[1:]:
        copy.wait()

    def halo_copies(it, into):
        return [
            remote(
                basis_ref.at[it], into.at[8 - c],
                halo_send.at[it, c], halo_recv.at[it, 8 - c], tile_at(c),
            )
            for c in sides
        ]

    eye_b = lax.broadcasted_iota(jnp.int32, (BLOCKS, BLOCKS), 0) == lax.broadcasted_iota(
        jnp.int32, (BLOCKS, BLOCKS), 1
    )
    count = jnp.sum(
        jnp.where(eye_b, count_ref[...].astype(f32), 0.0), axis=1, keepdims=True
    )
    lanes = lax.broadcasted_iota(jnp.int32, (BLOCKS, WIDTH), 1).astype(f32)
    live = (lanes < count).astype(f32)
    noise = noise_ref[...]
    precond = 1.0 / (noise + signal_amp)
    right_side = live * delta_ref[...]
    image_ref[0] = right_side
    basis_ref[0] = precond * right_side

    halo_refs = (halo0_ref, halo1_ref, halo2_ref)
    halo0_ref[OWN] = basis_ref[0]

    shape = (slots, slots)
    rows_s = lax.broadcasted_iota(jnp.int32, shape, 0)
    lanes_s = lax.broadcasted_iota(jnp.int32, shape, 1)
    codes = pair_ref[0]
    near_row = (codes >= 3).astype(jnp.int32) + (codes >= 6).astype(jnp.int32)
    row_s = me_s + near_row - 1
    row_g = me_g + (codes - 3 * near_row) - 1
    filled = codes < CODES
    inside = filled & (row_s >= 0) & (row_s < n_sky) & (row_g >= 0) & (row_g < n_gz)
    target = pair_ref[2]
    target_col = jnp.sum(jnp.where(rows_s == lanes_s, target, 0), axis=1, keepdims=True)
    before = (target < target_col) | ((target == target_col) & (lanes_s < rows_s))
    rank = jnp.sum(before.astype(jnp.int32), axis=1, keepdims=True)
    place = rank == lanes_s
    fields = (jnp.minimum(codes, CODES - 1), pair_ref[1], target, inside.astype(jnp.int32))
    limits = (CODES - 1, BLOCKS - 1, BLOCKS - 1, 1)
    table = jnp.zeros((SUB, slots), jnp.int32)
    for i, (field, limit) in enumerate(zip(fields, limits)):
        column = jnp.sum(jnp.where(rows_s == lanes_s, field, 0), axis=1, keepdims=True)
        moved = jnp.sum(jnp.where(place, column, 0), axis=0, keepdims=True)
        table = jnp.where(sub == i, jnp.clip(moved, 0, limit), table)
    ends = jnp.sum((target_col <= lanes_s).astype(jnp.int32), axis=0, keepdims=True)
    table = jnp.where(sub == len(fields), jnp.clip(ends, 0, slots), table)
    order_ref[...] = table
    to_scalar = pltpu.make_async_copy(order_ref, spair_ref, load_sem.at[5])
    to_scalar.start()

    flat = table[0:1] * BLOCKS + table[1:2]
    weight = table[3:4].astype(f32) * signal_amp
    hits = lax.broadcasted_iota(jnp.int32, (BLOCKS, slots), 0) == target
    named = jnp.sum(
        jnp.where(hits & filled, signal_amp, 0.0), axis=1, keepdims=True
    )
    rows_f = lax.broadcasted_iota(jnp.int32, (CODES * BLOCKS, slots), 0)
    backs = jnp.where(rows_f == flat, weight, 0.0)
    from_ref[:, :slots] = backs.astype(bf16)
    from_ref[:, slots:] = backs.astype(bf16)
    source_col = jnp.sum(
        jnp.where(rows_s == lanes_s, table[1:2], 0), axis=1, keepdims=True
    )
    by_code = jnp.where(
        lax.broadcasted_iota(jnp.int32, (2 * SUB, slots), 0) == table[0:1], weight, 0.0
    )
    sourced = mm(by_code.astype(bf16), (source_col == lanes_s).astype(bf16))
    for c in range(CODES):
        owed_ref[0, c, BLOCKS:] = jnp.broadcast_to(sourced[c : c + 1], (SUB, WIDTH))

    def spread(values):
        for block in range(BLOCKS):
            column_ref[block] = jnp.transpose(
                jnp.broadcast_to(values[block : block + 1], (WIDTH, WIDTH))
            )

    spread(basis_ref[0])

    def make_tile(slot, block, code, source):
        h, m, l = split_three(features(code, source, False))
        stack = jnp.concatenate([h, m, h, m, l, h], axis=0).astype(bf16)
        cov_ref[slot] = jnp.exp2(mm(near_ref[block, :, :depth], stack))

    def self_tile(step, _):
        for k in range(4):
            block = step * 4 + k
            make_tile(slots + block, block, OWN, block)
        return 0

    lax.fori_loop(0, BLOCKS // 4, self_tile, 0)
    to_scalar.wait()
    for copy in first:
        copy.wait_recv()
    arriving = halo_copies(0, halo0_ref)
    for copy in arriving:
        copy.start()

    def down(slot, block):
        product = cov_ref[slot] * column_ref[block]
        return jnp.sum(
            jnp.sum(product.reshape(WIDTH // SUB, SUB, WIDTH), axis=0), axis=0, keepdims=True
        )

    def doubled(values):
        high, low = split_two(values)
        return jnp.concatenate([high, low], axis=0)

    lanes_sq = lax.broadcasted_iota(jnp.int32, (WIDTH, WIDTH), 1)
    ones = jnp.ones((2 * WIDTH, WIDTH), bf16)
    def with_moment(moments, m):
        product = basis_ref[m // 2] * image_ref[m - m // 2]
        return jnp.where(sub == m, jnp.sum(product, axis=0, keepdims=True), moments)

    in_flight = first
    own_weight = None
    for it in range(ITERS):
        vector = basis_ref[it]
        halo_ref = halo_refs[it]
        if it > 0:
            arriving = halo_copies(it, halo_ref)
            for copy in arriving:
                copy.start()
            halo_ref[OWN] = vector

        if it > 0:
            spread(vector)

        if it == 0:

            def pair_tile(step, _):
                for k in range(64):
                    slot = step * 64 + k
                    make_tile(slot, spair_ref[2, slot], spair_ref[0, slot], spair_ref[1, slot])
                return 0

            lax.fori_loop(0, slots // 64, pair_tile, 0)

        def pay_step(step, _):
            total = jnp.zeros((SUB, WIDTH), f32)
            for k in range(SUB):
                slot = step * SUB + k
                total = jnp.where(sub == k, down(slot, spair_ref[2, slot]), total)
            pay_ref[pl.ds(step * SUB, SUB), :] = total
            return 0

        lax.fori_loop(0, slots // SUB, pay_step, 0)
        pays = doubled(pay_ref[...])
        extent = BLOCKS + SUB if it == 0 else BLOCKS
        returns = [
            remote(
                owed_ref.at[it, c, pl.ds(0, extent)], got_ref.at[it, 8 - c, pl.ds(0, extent)],
                owed_send.at[it, c], owed_recv.at[it, 8 - c], tile_at(c),
            )
            for c in sides
        ]
        for copy, c in zip(returns, sides):
            owed_ref[it, c, 0:BLOCKS] = mm(from_ref[c * BLOCKS : (c + 1) * BLOCKS], pays)
            copy.start()
        owed_ref[it, OWN, 0:BLOCKS] = mm(from_ref[OWN * BLOCKS : (OWN + 1) * BLOCKS], pays)

        def self_step(step, _):
            total = jnp.zeros((SUB, WIDTH), f32)
            for k in range(SUB):
                block = step * SUB + k
                total = jnp.where(sub == k, down(slots + block, block), total)
            self_ref[pl.ds(step * SUB, SUB), :] = total
            return 0

        lax.fori_loop(0, BLOCKS // SUB, self_step, 0)
        for copy in arriving:
            copy.wait_recv()

        def gain_step(step, running):
            for k in range(4 * SUB):
                slot = step * 4 * SUB + k
                row = halo_ref[spair_ref[0, slot], pl.ds(spair_ref[1, slot], 1), :]
                row = row * (spair_ref[3, slot].astype(f32) * signal_amp)
                same = spair_ref[2, slot] == spair_ref[2, jnp.maximum(slot - 1, 0)]
                running = running * same.astype(f32) + cov_ref[slot] * row
                running_ref[slot] = running
            return running

        lax.fori_loop(0, slots // SUB // 4, gain_step, jnp.zeros((WIDTH, WIDTH), f32))
        tall = jnp.zeros((WIDTH, WIDTH), f32)
        for block in range(BLOCKS):
            end = spair_ref[4, block]
            start = spair_ref[4, block - 1] if block > 0 else 0
            sums = running_ref[jnp.clip(end - 1, 0, slots - 1)]
            if block % 2 == 0:
                high, low = split_two(sums)
                reach = mm(jnp.concatenate([high, low], axis=1), ones)
            else:
                reach = jnp.sum(sums, axis=1, keepdims=True)
            reach = reach * (end > start).astype(f32)
            tall = jnp.where(lanes_sq == block, reach, tall)
        totals = jnp.transpose(tall)[:BLOCKS]
        totals = totals + owed_ref[it, OWN, 0:BLOCKS]
        if it == ITERS - 1:
            moments = jnp.zeros((SUB, WIDTH), f32)
            for m in range(2 * ITERS - 1):
                moments = with_moment(moments, m)
        for copy in returns:
            copy.wait_recv()
        for c in sides:
            totals = totals + got_ref[it, c, 0:BLOCKS]
        if it == 0:
            sources = owed_ref[0, OWN, BLOCKS:]
            for c in sides:
                sources = sources + got_ref[0, c, BLOCKS:]
            own_lane = lax.broadcasted_iota(
                jnp.int32, (BLOCKS, WIDTH), 0
            ) == lax.broadcasted_iota(jnp.int32, (BLOCKS, WIDTH), 1)
            own_weight = signal_amp + named + jnp.sum(
                jnp.where(own_lane, sources[0:1], 0.0), axis=1, keepdims=True
            )
        totals = totals + own_weight * self_ref[...]
        image = live * totals + noise * vector
        image_ref[it + 1] = image
        basis_ref[it + 1] = precond * image
        in_flight = in_flight + arriving + returns

    for m in range(2 * ITERS - 1, 2 * ITERS + 1):
        moments = with_moment(moments, m)
    stages = (
        (gz_at, n_gz, red1_ref, red1_send, red1_recv),
        (inner_at, INNER, red2_ref, red2_send, red2_recv),
        (outer_at, n_outer, red3_ref, red3_send, red3_recv),
    )
    for stage, (device_at, members, into, send, recv) in enumerate(stages):
        sum_ref[stage] = moments
        copies = [
            remote(
                sum_ref.at[stage], into.at[step - 1], send.at[step - 1], recv.at[step - 1],
                device_at(step),
            )
            for step in range(1, members)
        ]
        for copy in copies:
            copy.start()
        for copy in in_flight:
            copy.wait_send()
        in_flight = copies
        for step, copy in enumerate(copies):
            copy.wait_recv()
            moments = moments + into[step]
    total = jnp.sum(moments, axis=1, keepdims=True)
    mu = [total[m : m + 1] for m in range(2 * ITERS + 1)]

    def inner_product(left, right):
        value = None
        for i, a in enumerate(left):
            for j, b in enumerate(right):
                if a is not None and b is not None:
                    term = a * b * mu[i + j]
                    value = term if value is None else value + term
        return value

    def plus(left, scale, right):
        if right is None:
            return left
        return scale * right if left is None else left + scale * right

    one = jnp.ones((1, 1), f32)
    resid = [one, None, None, None]
    direct = [one, None, None, None]
    field = [None, None, None, None]
    rz = mu[0]
    for it in range(ITERS):
        moved = [None] + direct[:-1]
        alpha = rz / inner_product(direct, moved)
        field = [plus(a, alpha, b) for a, b in zip(field, direct)]
        resid = [plus(a, -alpha, b) for a, b in zip(resid, moved)]
        if it + 1 < ITERS:
            new = inner_product(resid, resid)
            beta = new / rz
            direct = [plus(a, beta, b) for a, b in zip(resid, direct)]
            rz = new
    out_field = field[0] * basis_ref[0]
    for i in range(1, ITERS):
        out_field = out_field + field[i] * basis_ref[i]
    out_resid = image_ref[0]
    for i in range(1, ITERS + 1):
        out_resid = out_resid + resid[i] * image_ref[i]
    out_ref[0] = out_field
    out_ref[1] = out_resid
    for copy in in_flight:
        copy.wait_send()


def local(delta_flux, noise_var, pixel_pos, pixel_count, pair_list):
    slots = pair_list.shape[3]
    n_sky = lax.axis_size("sky")
    n_gz = lax.axis_size("gz")
    n_outer = n_sky // INNER
    vmem = pl.BlockSpec(memory_space=pltpu.VMEM)
    hbm = pl.BlockSpec(memory_space=pltpu.HBM)
    shape = jax.ShapeDtypeStruct((2, BLOCKS, WIDTH), f32)
    dma = pltpu.SemaphoreType.DMA
    both = pl.pallas_call(
        functools.partial(body, slots),
        out_shape=shape,
        in_specs=[hbm] * 5,
        out_specs=vmem,
        scratch_shapes=[
            pltpu.VMEM((BLOCKS, WIDTH), f32),
            pltpu.VMEM((BLOCKS, WIDTH), f32),
            pltpu.VMEM((3, BLOCKS, WIDTH), f32),
            pltpu.VMEM((1, BLOCKS), jnp.int32),
            pltpu.VMEM((3, 1, slots), jnp.int32),
            pltpu.VMEM((SUB, slots), jnp.int32),
            pltpu.SMEM((SUB, slots), jnp.int32),
            pltpu.VMEM((BLOCKS, WIDTH, WIDTH), bf16),
            pltpu.VMEM((slots + BLOCKS, WIDTH, WIDTH), f32),
            pltpu.VMEM((slots, WIDTH, WIDTH), f32),
            pltpu.VMEM((BLOCKS, WIDTH, WIDTH), f32),
            pltpu.VMEM((CODES, 3, BLOCKS, WIDTH), f32),
            pltpu.VMEM((CODES, BLOCKS, WIDTH), f32),
            pltpu.VMEM((CODES, BLOCKS, WIDTH), f32),
            pltpu.VMEM((CODES, BLOCKS, WIDTH), f32),
            pltpu.VMEM((ITERS, CODES, BLOCKS + SUB, WIDTH), f32),
            pltpu.VMEM((ITERS, CODES, BLOCKS + SUB, WIDTH), f32),
            pltpu.VMEM((slots, WIDTH), f32),
            pltpu.VMEM((BLOCKS, WIDTH), f32),
            pltpu.VMEM((ITERS + 1, BLOCKS, WIDTH), f32),
            pltpu.VMEM((ITERS + 1, BLOCKS, WIDTH), f32),
            pltpu.VMEM((CODES * BLOCKS, 2 * slots), bf16),
            pltpu.VMEM((3, SUB, WIDTH), f32),
            pltpu.VMEM((n_gz - 1, SUB, WIDTH), f32),
            pltpu.VMEM((INNER - 1, SUB, WIDTH), f32),
            pltpu.VMEM((n_outer - 1, SUB, WIDTH), f32),
            dma((6,)), dma((CODES,)), dma((CODES,)),
            dma((ITERS, CODES)), dma((ITERS, CODES)),
            dma((ITERS, CODES)), dma((ITERS, CODES)),
            dma((n_gz - 1,)), dma((n_gz - 1,)),
            dma((INNER - 1,)), dma((INNER - 1,)),
            dma((n_outer - 1,)), dma((n_outer - 1,)),
        ],
        compiler_params=pltpu.CompilerParams(
            collective_id=0, has_side_effects=True, vmem_limit_bytes=40 * 1024 * 1024
        ),
    )(
        *(
            pltpu.with_memory_space_constraint(value, pltpu.HBM)
            for value in (
                delta_flux, noise_var, pixel_pos, pixel_count, jnp.transpose(pair_list, (0, 2, 1, 3))
            )
        )
    )
    return both[0][None, None], both[1][None, None]


def solution(mesh):
    placed = (
        P("sky", "gz", None, None),
        P("sky", "gz", None, None),
        P("sky", "gz", None, None, None),
        P("sky", "gz", None),
        P("sky", "gz", None, None),
    )
    return jax.shard_map(
        local,
        mesh=mesh,
        in_specs=placed,
        out_specs=(P("sky", "gz", None, None), P("sky", "gz", None, None)),
        check_vma=False,
    )
```
